32 devices in a mesh: groups: 2 (over x), replica: 8 (over z, y), channel: 2 (over core).
Axes of the slice: x: 2, y: 2, z: 4, core: 2. Of those that a mesh axis runs over, the one named last changes fastest.
Arguments:
- queries: bfloat16 [16, 2, 32, 4096], P(('groups', 'replica'), None, None, 'channel'), parts along dimension 0, may hold values from -360 to 360
- new_kv: bfloat16 [16, 2, 32, 1024], P(('groups', 'replica'), None, None, 'channel'), parts along dimension 0, may hold values from -6 to 6
- cached_lookup_pairs: bfloat16 [16, 1024, 1024], P(('groups', 'replica'), None, 'channel'), parts along dimension 0, may hold values from -6 to 6
- prefix_ssm: bfloat16 [16, 16, 8192], P(('groups', 'replica'), None, 'channel'), parts along dimension 0, may hold values from -6 to 6
- prefix_conv: bfloat16 [16, 3, 8192], P(('groups', 'replica'), None, 'channel'), parts along dimension 0, may hold values from -6 to 6
- pool_kv: bfloat16 [16, 4, 256, 1024], P(('groups', 'replica'), None, None, 'channel'), parts along dimension 0, may hold values from -6 to 6
- pool_ssm: bfloat16 [16, 16, 8192], P(('groups', 'replica'), None, 'channel'), parts along dimension 0, may hold values from -6 to 6
- pool_conv: bfloat16 [16, 3, 8192], P(('groups', 'replica'), None, 'channel'), parts along dimension 0, may hold values from -6 to 6
- owner_id: int32 [2], P('groups'), parts along dimension 0, may hold values from 0 to 7
- readers: int32 [16], P(('groups', 'replica')), parts along dimension 0, may hold values 0 or 1
- restore_src: int32 [16, 4], P('groups'), parts along dimension 0, may hold values from 0 to 7, as said below
- restore_blk: int32 [16, 4], P('groups'), parts along dimension 0, may hold values from 0 to 3, as said below
- state_src: int32 [16], P('groups'), parts along dimension 0, may hold values from 0 to 7, as said below
- ctx_blocks: int32 [16], P(('groups', 'replica')), parts along dimension 0, may hold values from 1 to 4, as said below
- mamba_x: bfloat16 [16, 2, 32, 8192], P(('groups', 'replica'), None, None, 'channel'), parts along dimension 0, may hold values from -6 to 6
- mamba_z: bfloat16 [16, 2, 32, 8192], P(('groups', 'replica'), None, None, 'channel'), parts along dimension 0, may hold values from -6 to 6
- mamba_dt: bfloat16 [16, 2, 32, 8192], P(('groups', 'replica'), None, None, 'channel'), parts along dimension 0, may hold values from -2 to 8
- dt_bias: float32 [8192], P('channel'), may hold values from -6 to -2.5
- a_log: float32 [16, 8192], P(None, 'channel'), may hold values from 0 to 2
- bypass_gain: float32 [8192], P('channel'), may hold values from 0.5 to 1.5
- conv_w: float32 [4, 8192], P(None, 'channel'), may hold values from -3 to 3
- conv_b: float32 [8192], P('channel'), may hold values from -0.5 to 0.5
- w_bc: bfloat16 [8192, 32], P('channel'), may hold values from -0.0625 to 0.0625
Outputs:
- attention_out: bfloat16 [16, 2, 32, 4096], P(('groups', 'replica'), None, None, 'channel'), parts along dimension 0
- mamba_out: bfloat16 [16, 2, 32, 8192], P(('groups', 'replica'), None, None, 'channel'), parts along dimension 0
The draws below stay inside these ranges and needn't reach their ends.
There are 2 independent parts, one for each index of `groups`. The reference program is written for one: setup_inputs(seed, part) draws one part's arguments, and reference() takes and returns one part's arrays. A program takes and returns all parts, laid end to end along the dimension named above; an argument that names none is the same for every part. Nothing has to cross between parts.
Inputs may be any that keep to these rules, and one draw needn't show every extreme that they name: `restore_src`: each row names 4 different replicas, and each replica is named in exactly 4 rows, so at most one block goes from one replica to one row's replica. Every pair (restore_src, restore_blk) is different: each stored block of each replica is listed exactly once. `state_src`: A permutation of the replicas. Only slots j < ctx_blocks[d] of row d are read; some replica has 4.
All inputs are finite; a program needn't handle non-finite values. No bound on the sum of `readers` on one device may be relied on, other than what follows from the above.
Results may differ from the reference program's by a relative error of at most 0.0049.
Values may be sent and summed in bfloat16 or wider, within the bound.
No kernel may reach another device: no remote copies, remote signals or barrier semaphores. Data moves between devices by JAX's collectives and lax.ppermute only.
A program may use at most 128 MiB of HBM per device.

```python
import jax
import jax.numpy as jnp
from jax import lax

HD = 128
KV_HEADS = 4
Q_PER_KV = 8
Q_HEADS = 32
KVW = 1024
INNER = 8192
STATE = 16
CONV = 4
BLOCK = 256
MAXB = 4
POOL = 4
PREFIX = 1024
NEW = 32
N_REPLICA = 8


def restore_tables(key):
    base = jax.random.fold_in(key, 7031)
    key_a, key_b, key_c, key_d = jax.random.split(base, 4)
    labels = jax.random.permutation(key_a, N_REPLICA)
    slots = jax.random.permutation(key_b, N_REPLICA)
    offsets = jax.random.permutation(key_c, N_REPLICA)[:MAXB]
    sources = labels[(slots[:, None] + offsets[None, :]) % N_REPLICA]
    orders = jax.vmap(lambda sub_key: jax.random.permutation(sub_key, MAXB))(jax.random.split(key_d, N_REPLICA))
    blocks = orders[sources, jnp.arange(MAXB)[None, :]]
    return (sources.astype(jnp.int32), blocks.astype(jnp.int32))


def draw_restore_src(key, part):
    return restore_tables(key)[0]


def draw_restore_blk(key, part):
    return restore_tables(key)[1]


def draw_state_src(key, part):
    return jax.random.permutation(jax.random.fold_in(key, 9127), N_REPLICA).astype(jnp.int32)


def draw_ctx_blocks(key, part):
    base = jax.random.fold_in(key, 4409)
    key_a, key_b = jax.random.split(base)
    payload_lines = jax.random.randint(key_a, (N_REPLICA,), MAXB - 3, MAXB + 1)
    chosen = jax.random.randint(key_b, (), 0, N_REPLICA)
    return jnp.where(jnp.arange(N_REPLICA) == chosen, MAXB, payload_lines).astype(jnp.int32)


def draw_queries(key, part):
    base = jax.random.fold_in(key, 2203)
    key_a = jax.random.fold_in(base, 0)
    payload_lines = jnp.clip(jax.random.normal(key_a, (N_REPLICA, 2, NEW, Q_HEADS * HD), jnp.float32), -6.0, 6.0)
    return payload_lines.astype(jnp.bfloat16)


def draw_mamba_dt(key, part):
    base = jax.random.fold_in(key, 5581)
    key_a, key_b = jax.random.split(base)
    shape = (N_REPLICA, 2, NEW, INNER)
    payload_lines = jnp.clip(0.5 * jax.random.normal(key_a, shape, jnp.float32), -2.0, 2.0)
    destination_places = jax.random.randint(key_b, (N_REPLICA, 2, 3), 0, NEW)
    update_order = jnp.arange(NEW)[None, None, None, :]
    copy_batches = jnp.sum((destination_places[..., None] == update_order).astype(jnp.float32), axis=2)
    return (payload_lines + 2.0 * copy_batches[..., None]).astype(jnp.bfloat16)


def plant(entries, rng, low, largest):
    longest = entries.shape.index(max(entries.shape))
    spots = []
    for shift in (0, 1):
        where = [jax.random.randint(jax.random.fold_in(rng, axis), (), 0, length) for axis, length in enumerate(entries.shape)]
        where[longest] = (where[longest] + shift) % entries.shape[longest]
        spots.append(tuple(where))
    return entries.at[spots[0]].set(low).at[spots[1]].set(largest)


def block_levels(own_key, shape, cuts, low, largest):
    loudness, own = 1.0, jax.random.fold_in(own_key, 6)
    for position, blocks in cuts:
        steps = jnp.exp(jax.random.uniform(jax.random.fold_in(own, position), (blocks,), jnp.float32, low / len(cuts), largest / len(cuts)))
        loudness = loudness * jnp.repeat(steps, shape[position] // blocks).reshape([-1 if axis == position else 1 for axis in range(len(shape))])
    return loudness


def noise(key, extent, deviation, limit, shards=(), kind=jnp.bfloat16):
    factor_of = block_levels(key, extent, shards, -0.22, 0.18) if shards else 1.0
    values = jax.random.normal(key, extent, jnp.float32) * deviation * factor_of
    return jnp.minimum(jnp.maximum(values, -limit), limit).astype(kind)


def setup_inputs(seed: int = 0, part: int = 0) -> dict:
    seeds = jax.random.split(jax.random.key(seed), 24)
    part_keys = jax.random.split(jax.random.fold_in(seeds[23], part), 24)
    queries = draw_queries(jax.random.fold_in(jax.random.fold_in(seeds[23], part), 71), part)
    new_kv = noise(part_keys[1], (N_REPLICA, 2, NEW, KVW), 1.0, 6.0, ((0, 8), (3, 2)))
    cached_lookup_pairs = noise(part_keys[2], (N_REPLICA, PREFIX, KVW), 1.0, 6.0, ((0, 8), (2, 2)))
    prefix_ssm = noise(part_keys[3], (N_REPLICA, STATE, INNER), 1.0, 6.0, ((0, 8), (2, 2)))
    prefix_conv = noise(part_keys[4], (N_REPLICA, CONV - 1, INNER), 1.0, 6.0, ((0, 8), (2, 2)))
    pool_kv = noise(part_keys[5], (N_REPLICA, POOL, BLOCK, KVW), 1.0, 6.0, ((0, 8), (3, 2)))
    pool_ssm = noise(part_keys[6], (N_REPLICA, STATE, INNER), 1.0, 6.0, ((0, 8), (2, 2)))
    pool_conv = noise(part_keys[7], (N_REPLICA, CONV - 1, INNER), 1.0, 6.0, ((0, 8), (2, 2)))
    owner_id = jax.random.randint(part_keys[8], (1,), 0, N_REPLICA).astype(jnp.int32)
    readers = plant((jax.random.randint(part_keys[9], (N_REPLICA,), 0, 4) < 3).astype(jnp.int32), jax.random.fold_in(part_keys[9], 1), 0, 1)
    restore_src = draw_restore_src(jax.random.fold_in(jax.random.fold_in(seeds[23], part), 71), part)
    restore_blk = draw_restore_blk(jax.random.fold_in(jax.random.fold_in(seeds[23], part), 71), part)
    state_src = draw_state_src(jax.random.fold_in(jax.random.fold_in(seeds[23], part), 71), part)
    ctx_blocks = draw_ctx_blocks(jax.random.fold_in(jax.random.fold_in(seeds[23], part), 71), part)
    mamba_x = noise(part_keys[14], (N_REPLICA, 2, NEW, INNER), 1.0, 6.0, ((0, 8), (3, 2)))
    mamba_z = noise(part_keys[15], (N_REPLICA, 2, NEW, INNER), 1.0, 6.0, ((0, 8), (3, 2)))
    mamba_dt = draw_mamba_dt(jax.random.fold_in(jax.random.fold_in(seeds[23], part), 71), part)
    dt_bias = jnp.clip(-6.0 + 3.5 * jax.random.uniform(seeds[17], (INNER,), jnp.float32) ** block_levels(seeds[17], (INNER,), ((0, 2),), -0.2, 0.2), -6.0, -2.5)
    a_log = jnp.clip(2.0 * jax.random.uniform(seeds[18], (STATE, INNER), jnp.float32) ** block_levels(seeds[18], (STATE, INNER), ((1, 2),), -0.2, 0.2), 0.0, 2.0)
    bypass_gain = jnp.clip(0.5 + 1.0 * jax.random.uniform(seeds[19], (INNER,), jnp.float32) ** block_levels(seeds[19], (INNER,), ((0, 2),), -0.2, 0.2), 0.5, 1.5)
    conv_w = noise(seeds[20], (CONV, INNER), CONV ** -0.5, 3.0, ((1, 2),), jnp.float32)
    conv_b = jnp.clip(jax.random.uniform(seeds[21], (INNER,), jnp.float32, -0.5, 0.5) * block_levels(seeds[21], (INNER,), ((0, 2),), -0.4, 0.0), -0.5, 0.5)
    w_bc = noise(seeds[22], (INNER, 2 * STATE), INNER ** -0.5, 0.0625, ((0, 2),))
    return {"queries": queries, "new_kv": new_kv, "cached_lookup_pairs": cached_lookup_pairs, "prefix_ssm": prefix_ssm, "prefix_conv": prefix_conv, "pool_kv": pool_kv, "pool_ssm": pool_ssm, "pool_conv": pool_conv, "owner_id": owner_id, "readers": readers, "restore_src": restore_src, "restore_blk": restore_blk, "state_src": state_src, "ctx_blocks": ctx_blocks, "mamba_x": mamba_x, "mamba_z": mamba_z, "mamba_dt": mamba_dt, "dt_bias": dt_bias, "a_log": a_log, "bypass_gain": bypass_gain, "conv_w": conv_w, "conv_b": conv_b, "w_bc": w_bc}


def attend(query_rows, context, live_keys, fresh_keys):
    factor = query_rows.shape[-1] ** -0.5
    rows_f = query_rows.astype(jnp.float32)
    scores_ctx = jnp.einsum("qhgd,khd->hgqk", rows_f, context[:, :, 0].astype(jnp.float32)) * factor
    scores_ctx = jnp.where(live_keys, scores_ctx, -jnp.inf)
    scores_new = jnp.einsum("qhgd,khd->hgqk", rows_f, fresh_keys[:, :, 0].astype(jnp.float32)) * factor
    new_count = fresh_keys.shape[0]
    causal = lax.broadcasted_iota(jnp.int32, (new_count, new_count), 0) >= lax.broadcasted_iota(jnp.int32, (new_count, new_count), 1)
    scores_new = jnp.where(causal, scores_new, -jnp.inf)
    highest = jnp.maximum(jnp.max(scores_ctx, axis=-1, keepdims=True), jnp.max(scores_new, axis=-1, keepdims=True))
    weight_ctx = jnp.exp(scores_ctx - highest)
    weight_new = jnp.exp(scores_new - highest)
    denominator = jnp.sum(weight_ctx, axis=-1) + jnp.sum(weight_new, axis=-1)
    scaled_product = jnp.einsum("hgqk,khd->qhgd", weight_ctx.astype(jnp.bfloat16).astype(jnp.float32), context[:, :, 1].astype(jnp.float32))
    scaled_product = scaled_product + jnp.einsum("hgqk,khd->qhgd", weight_new.astype(jnp.bfloat16).astype(jnp.float32), fresh_keys[:, :, 1].astype(jnp.float32))
    result = scaled_product / jnp.transpose(denominator, (2, 0, 1))[..., None]
    return result.astype(jnp.bfloat16).reshape(new_count, -1)


def reference(queries, new_kv, cached_lookup_pairs, prefix_ssm, prefix_conv, pool_kv, pool_ssm, pool_conv, owner_id, readers, restore_src, restore_blk, state_src, ctx_blocks, mamba_x, mamba_z, mamba_dt, dt_bias, a_log, bypass_gain, conv_w, conv_b, w_bc):
    owner_pos = owner_id[0]
    shared_kv = cached_lookup_pairs[owner_pos]
    shared_ssm = prefix_ssm[owner_pos].astype(jnp.float32)
    shared_conv = prefix_conv[owner_pos].astype(jnp.float32)
    decay_rate = -jnp.exp(a_log)
    w_bc_f = w_bc.astype(jnp.float32)

    def serve_one(replica_pos):
        reading_replica = readers[replica_pos] > 0
        grouped = queries[replica_pos].reshape(2, NEW, KV_HEADS, Q_PER_KV, HD)
        fresh_kv = new_kv[replica_pos].reshape(2, NEW, KV_HEADS, 2, HD)
        prefix_ctx = shared_kv.reshape(PREFIX, KV_HEADS, 2, HD)
        fresh_out = attend(grouped[0], prefix_ctx, jnp.broadcast_to(reading_replica, (PREFIX,)), fresh_kv[0])
        sources = restore_src[replica_pos]
        blocks = restore_blk[replica_pos]
        restored = pool_kv[sources, blocks].reshape(MAXB * BLOCK, KV_HEADS, 2, HD)
        live_keys = jnp.arange(MAXB * BLOCK, dtype=jnp.int32) < ctx_blocks[replica_pos] * BLOCK
        resumed_out = attend(grouped[1], restored, live_keys, fresh_kv[1])
        holder = state_src[replica_pos]
        start_ssm = jnp.stack([jnp.where(reading_replica, shared_ssm, 0.0), pool_ssm[holder].astype(jnp.float32)])
        start_conv = jnp.stack([jnp.where(reading_replica, shared_conv, 0.0), pool_conv[holder].astype(jnp.float32)])
        padded = jnp.concatenate([start_conv, mamba_x[replica_pos].astype(jnp.float32)], axis=1)
        conv_sum = conv_b + conv_w[0] * padded[:, 0:NEW]
        for offset in range(1, CONV):
            conv_sum = conv_sum + conv_w[offset] * padded[:, offset:offset + NEW]
        signal = jax.nn.silu(conv_sum)
        signal_round = lax.optimization_barrier(signal.astype(jnp.bfloat16)).astype(jnp.float32)
        state_bc = jnp.einsum("rtc,cs->rts", signal_round, w_bc_f)
        input_gain = state_bc[..., :STATE]
        readout = state_bc[..., STATE:]
        step_size = jax.nn.softplus(mamba_dt[replica_pos].astype(jnp.float32) + dt_bias)

        def advance(hidden, inputs):
            step_now, signal_now, gain_now, readout_now = inputs
            hidden = jnp.exp(step_now[:, None, :] * decay_rate) * hidden + gain_now[:, :, None] * (step_now * signal_now)[:, None, :]
            result = jnp.sum(readout_now[:, :, None] * hidden, axis=1) + bypass_gain * signal_now
            return hidden, result

        ignored, outputs = lax.scan(advance, start_ssm, (jnp.swapaxes(step_size, 0, 1), jnp.swapaxes(signal, 0, 1), jnp.swapaxes(input_gain, 0, 1), jnp.swapaxes(readout, 0, 1)))
        gated = (jnp.swapaxes(outputs, 0, 1) * jax.nn.silu(mamba_z[replica_pos].astype(jnp.float32))).astype(jnp.bfloat16)
        return jnp.stack([fresh_out, resumed_out]), gated

    attention_out, mamba_out = lax.map(serve_one, jnp.arange(N_REPLICA, dtype=jnp.int32))
    return attention_out, mamba_out
```

```python
import functools
import math

import jax
import jax.numpy as jnp
from jax import lax
from jax.experimental import pallas as pl
from jax.experimental.pallas import tpu as pltpu
from jax.sharding import PartitionSpec as P

HD = 128
Q_PER_KV = 8
F32 = jnp.float32
BF16 = jnp.bfloat16
LOG2E = math.log2(math.e)
SCORE2 = HD ** (-0.5) * LOG2E
LOW = -1e30
STAT = 16
VMEM_LIMIT = 48 * 1024 * 1024

VSPEC = pl.BlockSpec(memory_space=pltpu.VMEM)
SSPEC = pl.BlockSpec(memory_space=pltpu.SMEM)


def call(body, out_shape, specs, scratch=(), cost=None):
    return pl.pallas_call(
        body,
        out_shape=out_shape,
        in_specs=specs,
        out_specs=jax.tree.map(lambda _: VSPEC, out_shape),
        scratch_shapes=list(scratch),
        compiler_params=pltpu.CompilerParams(vmem_limit_bytes=VMEM_LIMIT),
        cost_estimate=cost,
    )


def dot(a, b, ca, cb):
    return lax.dot_general(a, b, (((ca,), (cb,)), ((), ())), preferred_element_type=F32)


def pieces(row, count):
    out = []
    for _ in range(count):
        part = row.astype(BF16).astype(F32)
        out.append(part)
        row = row - part
    return out


def stat_block(rows, width):
    index = lax.broadcasted_iota(jnp.int32, (STAT, width), 0)
    block = jnp.zeros((STAT, width), F32)
    for i, row in enumerate(rows):
        block = jnp.where(index == i, row, block)
    return block.astype(BF16)


def stats_of(part_ref, base, head):
    block = part_ref[base : base + STAT, :].astype(F32)
    o = 5 * head
    top = block[o : o + 1] + block[o + 1 : o + 2] + block[o + 2 : o + 3]
    total = block[o + 3 : o + 4] + block[o + 4 : o + 5]
    return top, total


def prefix_body(heads, spans, *refs):
    info, own, nbr = refs[:3]
    qs = refs[3 : 3 + spans]
    outs = refs[3 + spans : 3 + 2 * spans]
    kv = refs[3 + 2 * spans]
    here, mine = info[0], info[1]
    rows = heads * HD

    @pl.when(here == 1)
    def _():
        kv[...] = jnp.where(mine == 1, own[...], nbr[...])
        for q, out in zip(qs, outs):
            wide = Q_PER_KV * (q.shape[0] - STAT) // (2 * heads * Q_PER_KV)
            stats = []
            for h in range(heads):
                qh = q[h * wide : (h + 1) * wide, :]
                s = dot(kv[:, 2 * h * HD : (2 * h + 1) * HD], qh, 1, 1)
                m = jnp.max(s, axis=0, keepdims=True)
                p = jnp.exp2((s - m) * SCORE2)
                l = jnp.sum(p, axis=0, keepdims=True)
                o = dot(kv[:, (2 * h + 1) * HD : (2 * h + 2) * HD], p.astype(BF16), 0, 0)
                out[h * HD : (h + 1) * HD, :] = o.astype(BF16)
                stats += pieces(m, 3) + pieces(l, 2)
            out[rows:, :] = stat_block(stats, wide)

    @pl.when(here != 1)
    def _():
        for q, out in zip(qs, outs):
            wide = out.shape[1]
            out[:rows, :] = jnp.zeros((rows, wide), BF16)
            low = jnp.full((1, wide), LOW, F32)
            zero = jnp.zeros((1, wide), F32)
            out[rows:, :] = stat_block((pieces(low, 3) + [zero, zero]) * heads, wide)


def blocks_body(heads, spans, slots, pair, *refs):
    info, src, blk, own, nbr = refs[:5]
    qs = refs[5 : 5 + spans]
    outs = refs[5 + spans : 5 + 2 * spans]
    acc, top, tot = refs[5 + 2 * spans :]
    z, y = info[0], info[1]
    rows = heads * HD
    for k, (q, out) in enumerate(zip(qs, outs)):
        half = q.shape[0] - STAT
        wide = half // (2 * heads)
        reader = lax.rem(z + (spans - k), spans) * pair + y
        ctx = jnp.max(q[half:, :].astype(F32))
        acc[...] = jnp.zeros_like(acc)
        top[...] = jnp.full(top.shape, LOW, F32)
        tot[...] = jnp.zeros_like(tot)

        def slot(j, carry, q=q, half=half, wide=wide, reader=reader, ctx=ctx):
            source = src[reader, j]
            live = (source // pair == z) & (j.astype(F32) < ctx)

            @pl.when(live)
            def _():
                b = blk[reader, j]
                kv = jnp.where(lax.rem(source, pair) == y, own[b], nbr[b])
                for h in range(heads):
                    lo = half // 2 + h * wide
                    s = dot(kv[:, 2 * h * HD : (2 * h + 1) * HD], q[lo : lo + wide, :], 1, 1)
                    old = top[h]
                    m = jnp.maximum(old, jnp.max(s, axis=0, keepdims=True))
                    p = jnp.exp2((s - m) * SCORE2)
                    fade = jnp.exp2((old - m) * SCORE2)
                    o = dot(kv[:, (2 * h + 1) * HD : (2 * h + 2) * HD], p.astype(BF16), 0, 0)
                    acc[h] = acc[h] * fade + o
                    tot[h] = tot[h] * fade + jnp.sum(p, axis=0, keepdims=True)
                    top[h] = m

            return carry

        lax.fori_loop(0, slots, slot, 0)
        stats = []
        for h in range(heads):
            out[h * HD : (h + 1) * HD, :] = acc[h].astype(BF16)
            stats += pieces(top[h], 3) + pieces(tot[h], 2)
        out[rows:, :] = stat_block(stats, wide)


def join_body(heads, spans, *refs):
    flag, q, new = refs[:3]
    parts = (refs[3 : 3 + spans], refs[3 + spans : 3 + 2 * spans])
    out = refs[3 + 2 * spans]
    fresh = new.shape[1]
    half = q.shape[0] - STAT
    wide = half // (2 * heads)
    rows = heads * HD
    for r in range(2):
        for h in range(heads):
            lo = r * half // 2 + h * wide
            s = dot(new[r, :, 2 * h * HD : (2 * h + 1) * HD], q[lo : lo + wide, :], 1, 1)
            key = lax.broadcasted_iota(jnp.int32, (fresh, wide), 0)
            token = lax.rem(lax.broadcasted_iota(jnp.int32, (fresh, wide), 1), fresh)
            seen = key <= token
            s = jnp.where(seen, s, LOW)
            best = jnp.max(s, axis=0, keepdims=True)
            stats = [stats_of(part, rows, h) for part in parts[r]]
            if r == 0:
                stats = [(jnp.where(flag[0] > 0, m, LOW), l) for m, l in stats]
            for m, _ in stats:
                best = jnp.maximum(best, m)
            p = jnp.where(seen, jnp.exp2((s - best) * SCORE2), 0.0)
            total = jnp.sum(p, axis=0, keepdims=True)
            o = dot(new[r, :, (2 * h + 1) * HD : (2 * h + 2) * HD], p.astype(BF16), 0, 0)
            for part, (m, l) in zip(parts[r], stats):
                w = jnp.exp2((m - best) * SCORE2)
                total = total + w * l
                o = o + w * part[h * HD : (h + 1) * HD, :].astype(F32)
            done = jnp.transpose(o / total).astype(BF16)
            for g in range(Q_PER_KV):
                col = (h * Q_PER_KV + g) * HD
                out[r, :, col : col + HD] = done[g * fresh : (g + 1) * fresh, :]


def silu(x):
    return x / (1.0 + jnp.exp(-x))


def gains_body(state, chunk, flag, st0, st1, x, w, b, wbc, out, pad):
    taps = w.shape[0]
    keep = taps - 1
    length = x.shape[1]
    lead = 8
    total = [jnp.zeros((length, wbc.shape[1]), F32) for _ in range(2)]
    for c in range(0, x.shape[2], chunk):
        at = slice(c, c + chunk)
        for r, st in enumerate((st0, st1)):
            first = st[state : state + keep, at].astype(F32)
            if r == 0:
                first = jnp.where(flag[0] > 0, first, 0.0)
            pad[r, lead - keep : lead, :] = first
            pad[r, lead:, :] = x[r, :, at].astype(F32)
            acc = b[:, at] + w[0:1, at] * pad[r, lead - keep : lead - keep + length, :]
            for k in range(1, taps):
                acc = acc + w[k : k + 1, at] * pad[r, lead - keep + k : lead - keep + k + length, :]
            total[r] = total[r] + dot(silu(acc).astype(BF16), wbc[at, :], 1, 0)
    for r in range(2):
        out[r] = total[r]


def scan_body(state, flag, bc, st0, st1, x, dt, zg, dtb, alog, gain, w, b, out, pad, step, push, res, dec):
    taps = w.shape[0]
    keep = taps - 1
    length = x.shape[1]
    sub = x.shape[2]
    block = 16
    dec[...] = jnp.exp(alog[...]) * (-LOG2E)
    for r, st in enumerate((st0, st1)):
        first = st[state : state + keep].astype(F32)
        if r == 0:
            first = jnp.where(flag[0] > 0, first, 0.0)
        pad[0:keep] = first
        pad[keep:] = x[r].astype(F32)

        def prepare(t, carry, r=r):
            acc = b[...] + w[0] * pad[t]
            for k in range(1, taps):
                acc = acc + w[k] * pad[t + k]
            sig = silu(acc)
            raw = dt[r, t].astype(F32) + dtb[...]
            now = jnp.maximum(raw, 0.0) + jnp.log1p(jnp.exp(-jnp.abs(raw)))
            step[r, t] = now
            push[r, t] = now * sig
            res[r, t] = gain[...] * sig
            return carry

        lax.fori_loop(0, length, prepare, 0)

    for r, st in enumerate((st0, st1)):
        for c in range(0, sub, block):
            at = slice(c, c + block)
            start = []
            for n in range(state):
                h = st[n, at, :].astype(F32)
                if r == 0:
                    h = jnp.where(flag[0] > 0, h, 0.0)
                start.append(h)

            def advance(t, hs, r=r, at=at):
                now = step[r, t, at, :]
                add = push[r, t, at, :]
                sums = [res[r, t, at, :], None, None, None]
                after = []
                for n in range(state):
                    h = jnp.exp2(now * dec[n, at, :]) * hs[n] + bc[r * length + t, n] * add
                    term = bc[r * length + t, state + n] * h
                    i = n % 4
                    sums[i] = term if sums[i] is None else sums[i] + term
                    after.append(h)
                y = (sums[0] + sums[1]) + (sums[2] + sums[3])
                gate = silu(zg[r, t, at, :].astype(F32))
                out[r, t, at, :] = (y * gate).astype(BF16)
                return tuple(after)

            lax.fori_loop(0, length, advance, tuple(start))


def local(
    size,
    queries,
    new_kv,
    cached_lookup_pairs,
    prefix_ssm,
    prefix_conv,
    pool_kv,
    pool_ssm,
    pool_conv,
    owner_id,
    readers,
    restore_src,
    restore_blk,
    state_src,
    ctx_blocks,
    mamba_x,
    mamba_z,
    mamba_dt,
    dt_bias,
    a_log,
    bypass_gain,
    conv_w,
    conv_b,
    w_bc,
):
    axis = "replica"
    pair = 2
    spans = size // pair
    length = queries.shape[2]
    heads = new_kv.shape[3] // (2 * HD)
    wide = Q_PER_KV * length
    slots = restore_src.shape[1]
    inner = mamba_x.shape[3]
    state = a_log.shape[0]
    keep = prefix_conv.shape[1]
    me = lax.axis_index(axis)
    z, y = me // pair, me % pair
    owner = owner_id[0]

    def across(value):
        return lax.ppermute(value, axis, [(s, s ^ 1) for s in range(size)])

    def turn(value, k):
        return lax.ppermute(value, axis, [(s, (s + k * pair) % size) for s in range(size)])

    states = jnp.concatenate([pool_ssm[0], pool_conv[0], prefix_ssm[0], prefix_conv[0]], axis=0)
    states_nbr = across(states)

    folded = queries[0].reshape(2, length, heads * Q_PER_KV, HD).transpose(0, 2, 1, 3)
    folded = folded.reshape(2 * heads * wide, HD)
    length_rows = jnp.full((STAT, HD), ctx_blocks[0].astype(BF16), BF16)
    message = jnp.concatenate([folded, length_rows], axis=0)
    asked = [message] + [turn(message, k) for k in range(1, spans)]

    prefix_nbr = across(cached_lookup_pairs[0])
    pool_nbr = across(pool_kv[0])

    part_shape = jax.ShapeDtypeStruct((heads * HD + STAT, wide), BF16)
    info0 = jnp.stack([(owner // pair == z), (owner % pair == y)]).astype(jnp.int32)
    keys = cached_lookup_pairs.shape[1]
    part0 = call(
        functools.partial(prefix_body, heads, spans),
        [part_shape] * spans,
        [SSPEC] + [VSPEC] * (2 + spans),
        [pltpu.VMEM(cached_lookup_pairs.shape[1:], BF16)],
        pl.CostEstimate(flops=spans * heads * keys * wide * HD * 4, bytes_accessed=4 << 20, transcendentals=spans * heads * keys * wide),
    )(info0, cached_lookup_pairs[0], prefix_nbr, *asked)
    got0 = [part0[0]] + [turn(part0[k], spans - k) for k in range(1, spans)]

    info1 = jnp.stack([z, y]).astype(jnp.int32)
    block_len = pool_kv.shape[2]
    part1 = call(
        functools.partial(blocks_body, heads, spans, slots, pair),
        [part_shape] * spans,
        [SSPEC] * 3 + [VSPEC] * (2 + spans),
        [
            pltpu.VMEM((heads, HD, wide), F32),
            pltpu.VMEM((heads, 1, wide), F32),
            pltpu.VMEM((heads, 1, wide), F32),
        ],
        pl.CostEstimate(flops=slots * heads * block_len * wide * HD * 4, bytes_accessed=4 << 20, transcendentals=slots * heads * block_len * wide),
    )(info1, restore_src, restore_blk, pool_kv[0], pool_nbr, *asked)
    got1 = [part1[0]] + [turn(part1[k], spans - k) for k in range(1, spans)]

    rows = state + keep

    def stored(holder):
        return jnp.where(holder % pair == y, states[:rows], states_nbr[:rows])

    back = [stored(state_src[me])]
    for k in range(1, spans):
        reader = ((z + k) % spans) * pair + y
        back.append(turn(stored(state_src[reader]), k))
    came = (z - state_src[me] // pair) % spans
    state1 = back[0]
    for k in range(1, spans):
        state1 = jnp.where(came == k, back[k], state1)
    state0 = jnp.where(owner % pair == y, states[rows:], states_nbr[rows:])
    away = owner // pair
    hop = 1
    while hop < spans:
        other = lax.ppermute(
            state0, axis, [(s, ((s // pair) ^ hop) * pair + s % pair) for s in range(size)]
        )
        state0 = jnp.where((away ^ z) & hop != 0, other, state0)
        hop *= 2

    chunk = math.gcd(inner, 512)
    partial = call(
        functools.partial(gains_body, state, chunk),
        jax.ShapeDtypeStruct((2, length, w_bc.shape[1]), F32),
        [SSPEC] + [VSPEC] * 6,
        [pltpu.VMEM((2, length + 8, chunk), F32)],
        pl.CostEstimate(flops=2 * 2 * length * inner * 32, bytes_accessed=2 << 20, transcendentals=2 * length * inner),
    )(readers, state0, state1, mamba_x[0], conv_w, conv_b[None], w_bc)
    both = partial + lax.ppermute(partial, "channel", [(0, 1), (1, 0)])
    bc = both.reshape(2 * length, w_bc.shape[1])
    sub = inner // HD

    def tiled(value):
        return value.reshape(value.shape[:-1] + (sub, HD))

    scan_out = call(
        functools.partial(scan_body, state),
        jax.ShapeDtypeStruct((2, length, sub, HD), BF16),
        [SSPEC] * 2 + [VSPEC] * 10,
        [
            pltpu.VMEM((length + keep, sub, HD), F32),
            pltpu.VMEM((2, length, sub, HD), F32),
            pltpu.VMEM((2, length, sub, HD), F32),
            pltpu.VMEM((2, length, sub, HD), F32),
            pltpu.VMEM((state, sub, HD), F32),
        ],
        pl.CostEstimate(flops=2 * length * inner * state * 6, bytes_accessed=4 << 20, transcendentals=2 * length * inner * state),
    )(
        readers,
        bc,
        tiled(state0),
        tiled(state1),
        tiled(mamba_x[0]),
        tiled(mamba_dt[0]),
        tiled(mamba_z[0]),
        tiled(dt_bias),
        tiled(a_log),
        tiled(bypass_gain),
        tiled(conv_w),
        tiled(conv_b),
    )
    mamba_out = scan_out.reshape(1, 2, length, inner)

    attention_out = call(
        functools.partial(join_body, heads, spans),
        jax.ShapeDtypeStruct((2, length, heads * Q_PER_KV * HD), BF16),
        [SSPEC] + [VSPEC] * (2 + 2 * spans),
        (),
        pl.CostEstimate(flops=1 << 24, bytes_accessed=2 << 20, transcendentals=1 << 16),
    )(readers, message, new_kv[0], *got0, *got1)[None]
    return (attention_out, mamba_out)


def solution(mesh):
    row = ("groups", "replica")
    placed = (
        P(row, None, None, "channel"),
        P(row, None, None, "channel"),
        P(row, None, "channel"),
        P(row, None, "channel"),
        P(row, None, "channel"),
        P(row, None, None, "channel"),
        P(row, None, "channel"),
        P(row, None, "channel"),
        P("groups"),
        P(row),
        P("groups", None),
        P("groups", None),
        P("groups"),
        P(row),
        P(row, None, None, "channel"),
        P(row, None, None, "channel"),
        P(row, None, None, "channel"),
        P("channel"),
        P(None, "channel"),
        P("channel"),
        P(None, "channel"),
        P("channel"),
        P("channel", None),
    )
    return jax.shard_map(
        functools.partial(local, mesh.shape["replica"]),
        mesh=mesh,
        in_specs=placed,
        out_specs=(P(row, None, None, "channel"), P(row, None, None, "channel")),
        check_vma=False,
    )
```

```python
import functools
import math

import jax
import jax.numpy as jnp
from jax import lax
from jax.experimental import pallas as pl
from jax.experimental.pallas import tpu as pltpu
from jax.sharding import PartitionSpec as P

HD = 128
Q_PER_KV = 8
F32 = jnp.float32
BF16 = jnp.bfloat16
LOG2E = math.log2(math.e)
SCORE2 = HD ** (-0.5) * LOG2E
LOW = -1e30
STAT = 16
VMEM_LIMIT = 48 * 1024 * 1024

VSPEC = pl.BlockSpec(memory_space=pltpu.VMEM)
SSPEC = pl.BlockSpec(memory_space=pltpu.SMEM)


def call(body, out_shape, specs, scratch=(), cost=None):
    return pl.pallas_call(
        body,
        out_shape=out_shape,
        in_specs=specs,
        out_specs=jax.tree.map(lambda _: VSPEC, out_shape),
        scratch_shapes=list(scratch),
        compiler_params=pltpu.CompilerParams(vmem_limit_bytes=VMEM_LIMIT),
        cost_estimate=cost,
    )


def dot(a, b, ca, cb):
    return lax.dot_general(a, b, (((ca,), (cb,)), ((), ())), preferred_element_type=F32)


def pieces(row, count):
    out = []
    for _ in range(count):
        part = row.astype(BF16).astype(F32)
        out.append(part)
        row = row - part
    return out


def stat_block(rows, width):
    index = lax.broadcasted_iota(jnp.int32, (STAT, width), 0)
    block = jnp.zeros((STAT, width), F32)
    for i, row in enumerate(rows):
        block = jnp.where(index == i, row, block)
    return block.astype(BF16)


def stats_of(part_ref, base, head):
    block = part_ref[base : base + STAT, :].astype(F32)
    o = 5 * head
    top = block[o : o + 1] + block[o + 1 : o + 2] + block[o + 2 : o + 3]
    total = block[o + 3 : o + 4] + block[o + 4 : o + 5]
    return top, total


def prefix_body(heads, spans, pair, *refs):
    me, owner, own, nbr = refs[:4]
    qs = refs[4 : 4 + spans]
    outs = refs[4 + spans : 4 + 2 * spans]
    kv = refs[4 + 2 * spans]
    here = owner[0] // pair == me[0] // pair
    rows = heads * HD

    @pl.when(here)
    def _():
        kv[...] = jnp.where(owner[0] == me[0], own[...], nbr[...])
        for q, out in zip(qs, outs):
            wide = Q_PER_KV * (q.shape[0] - STAT) // (2 * heads * Q_PER_KV)
            stats = []
            for h in range(heads):
                qh = q[h * wide : (h + 1) * wide, :]
                s = dot(kv[:, 2 * h * HD : (2 * h + 1) * HD], qh, 1, 1)
                m = jnp.max(s, axis=0, keepdims=True)
                p = jnp.exp2((s - m) * SCORE2)
                l = jnp.sum(p, axis=0, keepdims=True)
                o = dot(kv[:, (2 * h + 1) * HD : (2 * h + 2) * HD], p.astype(BF16), 0, 0)
                out[h * HD : (h + 1) * HD, :] = o.astype(BF16)
                stats += pieces(m, 3) + pieces(l, 2)
            out[rows:, :] = stat_block(stats, wide)

    @pl.when(jnp.logical_not(here))
    def _():
        for q, out in zip(qs, outs):
            wide = out.shape[1]
            out[:rows, :] = jnp.zeros((rows, wide), BF16)
            low = jnp.full((1, wide), LOW, F32)
            zero = jnp.zeros((1, wide), F32)
            out[rows:, :] = stat_block((pieces(low, 3) + [zero, zero]) * heads, wide)


def blocks_body(head, spans, slots, pair, *refs):
    me, src, blk, own, nbr = refs[:5]
    qs = refs[5 : 5 + spans]
    outs = refs[5 + spans : 5 + 2 * spans]
    acc, top, tot = refs[5 + 2 * spans :]
    z, y = me[0] // pair, lax.rem(me[0], pair)
    for k, (q, out) in enumerate(zip(qs, outs)):
        full = q.shape[0] - STAT
        wide = out.shape[1]
        lo = full // 2 + head * wide
        reader = lax.rem(z + (spans - k), spans) * pair + y
        ctx = jnp.max(q[full:, :].astype(F32))
        acc[...] = jnp.zeros_like(acc)
        top[...] = jnp.full(top.shape, LOW, F32)
        tot[...] = jnp.zeros_like(tot)

        def slot(j, carry, q=q, lo=lo, wide=wide, reader=reader, ctx=ctx):
            source = src[reader, j]
            live = (source // pair == z) & (j.astype(F32) < ctx)

            @pl.when(live)
            def _():
                b = blk[reader, j]
                kv = jnp.where(lax.rem(source, pair) == y, own[b, :, 2 * head * HD : 2 * (head + 1) * HD], nbr[b])
                s = dot(kv[:, :HD], q[lo : lo + wide, :], 1, 1)
                old = top[...]
                m = jnp.maximum(old, jnp.max(s, axis=0, keepdims=True))
                p = jnp.exp2((s - m) * SCORE2)
                fade = jnp.exp2((old - m) * SCORE2)
                o = dot(kv[:, HD:], p.astype(BF16), 0, 0)
                acc[...] = acc[...] * fade + o
                tot[...] = tot[...] * fade + jnp.sum(p, axis=0, keepdims=True)
                top[...] = m

            return carry

        lax.fori_loop(0, slots, slot, 0)
        out[:HD, :] = acc[...].astype(BF16)
        out[HD:, :] = stat_block(pieces(top[...], 3) + pieces(tot[...], 2), wide)


def join_body(heads, spans, *refs):
    flag, q, new = refs[:3]
    parts = [refs[3 + i * spans : 3 + (i + 1) * spans] for i in range(1 + heads)]
    out = refs[3 + (1 + heads) * spans]
    fresh = new.shape[1]
    half = q.shape[0] - STAT
    wide = half // (2 * heads)
    rows = heads * HD
    for r in range(2):
        for h in range(heads):
            lo = r * half // 2 + h * wide
            s = dot(new[r, :, 2 * h * HD : (2 * h + 1) * HD], q[lo : lo + wide, :], 1, 1)
            key = lax.broadcasted_iota(jnp.int32, (fresh, wide), 0)
            token = lax.rem(lax.broadcasted_iota(jnp.int32, (fresh, wide), 1), fresh)
            seen = key <= token
            s = jnp.where(seen, s, LOW)
            best = jnp.max(s, axis=0, keepdims=True)
            mine, at, base, place = (parts[0], h * HD, rows, h) if r == 0 else (parts[1 + h], 0, HD, 0)
            stats = [stats_of(part, base, place) for part in mine]
            if r == 0:
                stats = [(jnp.where(flag[0] > 0, m, LOW), l) for m, l in stats]
            for m, _ in stats:
                best = jnp.maximum(best, m)
            p = jnp.where(seen, jnp.exp2((s - best) * SCORE2), 0.0)
            total = jnp.sum(p, axis=0, keepdims=True)
            o = dot(new[r, :, (2 * h + 1) * HD : (2 * h + 2) * HD], p.astype(BF16), 0, 0)
            for part, (m, l) in zip(mine, stats):
                w = jnp.exp2((m - best) * SCORE2)
                total = total + w * l
                o = o + w * part[at : at + HD, :].astype(F32)
            done = jnp.transpose(o / total).astype(BF16)
            for g in range(Q_PER_KV):
                col = (h * Q_PER_KV + g) * HD
                out[r, :, col : col + HD] = done[g * fresh : (g + 1) * fresh, :]


def reach(away, spans, rounds, here):
    low = high = away
    for r in range(rounds):
        odd = r % 2
        below = jnp.where((lax.rem(low, 2) != odd) & (low > 0), low - 1, low)
        above = jnp.where((lax.rem(high, 2) == odd) & (high < spans - 1), high + 1, high)
        low, high = below, above
    return (low <= here) & (here <= high)


def shared_body(spans, pair, unit, rounds, me, owner, kept, came, out):
    z, y = me[0] // pair, lax.rem(me[0], pair)
    if rounds == 0:
        take = lax.rem(owner[0], pair) != y
        base = unit
    else:
        away = owner[0] // pair
        take = jnp.logical_not(reach(away, spans, rounds - 1, z))
        base = 0
    out[...] = jnp.where(take, came[base:, :], kept[base:, :])


def state_send_body(spans, pair, unit, me, src, own, nbr, *outs):
    z, y = me[0] // pair, lax.rem(me[0], pair)
    for k, out in enumerate(outs):
        source = src[lax.rem(z + k, spans) * pair + y]
        out[...] = jnp.where(lax.rem(source, pair) == y, own[:unit, :], nbr[:unit, :])


def state_take_body(spans, pair, me, src, *refs):
    came, out = refs[:spans], refs[spans]
    z = me[0] // pair
    k1 = lax.rem(z + spans - src[me[0]] // pair, spans)
    for k in range(spans):

        @pl.when(k1 == k)
        def _(k=k):
            out[...] = came[k][...]


def silu(x):
    return x / (1.0 + jnp.exp(-x))


def gains_body(chunk, flag, st0, st1, x, w, b, wbc, out, pad):
    taps = w.shape[0]
    keep = taps - 1
    length = x.shape[1]
    lead = 8
    total = [jnp.zeros((length, wbc.shape[0]), F32) for _ in range(2)]
    for c in range(0, x.shape[2], chunk):
        at = slice(c, c + chunk)
        for r, st in enumerate((st0, st1)):
            first = st[:, at].astype(F32)
            if r == 0:
                first = jnp.where(flag[0] > 0, first, 0.0)
            pad[r, lead - keep : lead, :] = first
            pad[r, lead:, :] = x[r, :, at].astype(F32)
            acc = b[:, at] + w[0:1, at] * pad[r, lead - keep : lead - keep + length, :]
            for k in range(1, taps):
                acc = acc + w[k : k + 1, at] * pad[r, lead - keep + k : lead - keep + k + length, :]
            total[r] = total[r] + dot(silu(acc).astype(BF16), wbc[:, at], 1, 1)
    for r in range(2):
        out[r] = total[r]


def scan_body(state, flag, bc, st0, st1, x, dt, zg, dtb, alog, gain, w, b, out, pad, step, push, res, dec):
    taps = w.shape[0]
    keep = taps - 1
    length = x.shape[1]
    sub = x.shape[2]
    block = 16
    dec[...] = jnp.exp(alog[...]) * (-LOG2E)
    for r, st in enumerate((st0, st1)):
        first = st[state : state + keep].astype(F32)
        if r == 0:
            first = jnp.where(flag[0] > 0, first, 0.0)
        pad[0:keep] = first
        pad[keep:] = x[r].astype(F32)

        def prepare(t, carry, r=r):
            acc = b[...] + w[0] * pad[t]
            for k in range(1, taps):
                acc = acc + w[k] * pad[t + k]
            sig = silu(acc)
            raw = dt[r, t].astype(F32) + dtb[...]
            now = jnp.maximum(raw, 0.0) + jnp.log1p(jnp.exp(-jnp.abs(raw)))
            step[r, t] = now
            push[r, t] = now * sig
            res[r, t] = gain[...] * sig
            return carry

        lax.fori_loop(0, length, prepare, 0)

    for r, st in enumerate((st0, st1)):
        for c in range(0, sub, block):
            at = slice(c, c + block)
            start = []
            for n in range(state):
                h = st[n, at, :].astype(F32)
                if r == 0:
                    h = jnp.where(flag[0] > 0, h, 0.0)
                start.append(h)

            def advance(t, hs, r=r, at=at):
                now = step[r, t, at, :]
                add = push[r, t, at, :]
                sums = [res[r, t, at, :], None, None, None]
                after = []
                for n in range(state):
                    h = jnp.exp2(now * dec[n, at, :]) * hs[n] + bc[r * length + t, n] * add
                    term = bc[r * length + t, state + n] * h
                    i = n % 4
                    sums[i] = term if sums[i] is None else sums[i] + term
                    after.append(h)
                y = (sums[0] + sums[1]) + (sums[2] + sums[3])
                gate = silu(zg[r, t, at, :].astype(F32))
                out[r, t, at, :] = (y * gate).astype(BF16)
                return tuple(after)

            lax.fori_loop(0, length, advance, tuple(start))


def local(
    size,
    queries,
    new_kv,
    cached_lookup_pairs,
    prefix_ssm,
    prefix_conv,
    pool_kv,
    pool_ssm,
    pool_conv,
    owner_id,
    readers,
    restore_src,
    restore_blk,
    state_src,
    ctx_blocks,
    mamba_x,
    mamba_z,
    mamba_dt,
    dt_bias,
    a_log,
    bypass_gain,
    conv_w,
    conv_b,
    w_bc,
):
    axis = "replica"
    pair = 2
    spans = size // pair
    length = queries.shape[2]
    heads = new_kv.shape[3] // (2 * HD)
    wide = Q_PER_KV * length
    slots = restore_src.shape[1]
    inner = mamba_x.shape[3]
    state = a_log.shape[0]
    keep = prefix_conv.shape[1]
    me = lax.axis_index(axis)[None]

    def across(value):
        return lax.ppermute(value, axis, [(s, s ^ 1) for s in range(size)])

    def turn(value, k):
        return lax.ppermute(value, axis, [(s, (s + k * pair) % size) for s in range(size)])

    def after(value, *others):
        return lax.optimization_barrier((value, *others))[0]

    sub = inner // HD

    def tiled(value):
        return value.reshape(value.shape[:-1] + (sub, HD))

    cols = 2 * HD
    rows = state + keep
    unit = rows * inner // cols
    states = jnp.concatenate([pool_ssm[0], pool_conv[0], prefix_ssm[0], prefix_conv[0]], axis=0)
    states = states.reshape(2 * unit, cols)
    states_nbr = across(states)

    folded = queries[0].reshape(2, length, heads * Q_PER_KV, HD).transpose(0, 2, 1, 3)
    folded = folded.reshape(2 * heads * wide, HD)
    length_rows = jnp.full((STAT, HD), ctx_blocks[0].astype(BF16), BF16)
    message = jnp.concatenate([folded, length_rows], axis=0)
    asked = [message] + [turn(message, k) for k in range(1, spans)]

    x_t, dt_t, z_t = tiled(mamba_x[0]), tiled(mamba_dt[0]), tiled(mamba_z[0])
    halves = [pool_kv[0, :, :, h * cols : (h + 1) * cols] for h in range(heads)]
    prefix_nbr = across(cached_lookup_pairs[0])

    one = jax.ShapeDtypeStruct((unit, cols), BF16)

    def shared(rounds, kept, came):
        return call(
            functools.partial(shared_body, spans, pair, unit, rounds),
            one,
            [SSPEC] * 2 + [VSPEC] * 2,
        )(me, owner_id, kept, came)

    def hop(value, r):
        odd = r % 2
        near = [(i, i + 1) for i in range(odd, spans - 1, 2)]
        links = [(pair * u + j, pair * v + j) for i, n in near for u, v in ((i, n), (n, i)) for j in range(pair)]
        return lax.ppermute(value, axis, links)

    state0 = shared(0, states, states_nbr)
    hops = [hop(state0, 0)] if spans > 1 else []

    sent = call(
        functools.partial(state_send_body, spans, pair, unit),
        [one] * spans,
        [SSPEC] * 2 + [VSPEC] * 2,
        (),
        pl.CostEstimate(flops=50 * 10**9, bytes_accessed=150 * 10**6, transcendentals=0),
    )(after(me, x_t, dt_t, z_t, *halves, *asked[1:], *hops[:1]), state_src, states, states_nbr)
    came = [sent[0]] + [turn(sent[k], k) for k in range(1, spans)]
    state1 = call(
        functools.partial(state_take_body, spans, pair),
        one,
        [SSPEC] * 2 + [VSPEC] * spans,
    )(me, state_src, *came)
    part_shape = jax.ShapeDtypeStruct((heads * HD + STAT, wide), BF16)
    keys = cached_lookup_pairs.shape[1]
    part0 = call(
        functools.partial(prefix_body, heads, spans, pair),
        [part_shape] * spans,
        [SSPEC] * 2 + [VSPEC] * (2 + spans),
        [pltpu.VMEM(cached_lookup_pairs.shape[1:], BF16)],
        pl.CostEstimate(flops=50 * 10**9, bytes_accessed=150 * 10**6, transcendentals=0),
    )(me, owner_id, cached_lookup_pairs[0], prefix_nbr, *asked)
    for r in range(1, spans):
        state0 = shared(r, state0, hops[-1])
        if r < spans - 1:
            hops.append(hop(after(state0, part0[0]), r))
    got0 = [part0[0]] + [turn(part0[k], spans - k) for k in range(1, spans)]

    block_len = pool_kv.shape[2]
    head_shape = jax.ShapeDtypeStruct((HD + STAT, wide), BF16)
    got1 = []
    last = [sent[0]]
    for h in range(heads):
        pool_nbr = across(after(halves[h], *last))
        last = [pool_nbr, part0[0]]
        part1 = call(
            functools.partial(blocks_body, h, spans, slots, pair),
            [head_shape] * spans,
            [SSPEC] * 3 + [VSPEC] * (2 + spans),
            [pltpu.VMEM((HD, wide), F32), pltpu.VMEM((1, wide), F32), pltpu.VMEM((1, wide), F32)],
            pl.CostEstimate(flops=20 * 10**9, bytes_accessed=60 * 10**6, transcendentals=0),
        )(after(me, part0[0], *(got0[1:] if h else ())), restore_src, restore_blk, pool_kv[0], pool_nbr, *asked)
        got1 += [part1[0]] + [turn(part1[k], spans - k) for k in range(1, spans)]

    first = state * inner // cols

    def taps_of(value):
        return value[first:].reshape(keep, inner)

    chunk = math.gcd(inner, 512)
    partial = call(
        functools.partial(gains_body, chunk),
        jax.ShapeDtypeStruct((2, length, w_bc.shape[1]), F32),
        [SSPEC] + [VSPEC] * 6,
        [pltpu.VMEM((2, length + 8, chunk), F32)],
        pl.CostEstimate(flops=2 * 2 * length * inner * 32, bytes_accessed=2 << 20, transcendentals=2 * length * inner),
    )(readers, taps_of(state0), taps_of(state1), mamba_x[0], conv_w, conv_b[None], w_bc.T)
    both = partial + lax.ppermute(partial, "channel", [(0, 1), (1, 0)])
    bc = both.reshape(2 * length, w_bc.shape[1])
    scan_out = call(
        functools.partial(scan_body, state),
        jax.ShapeDtypeStruct((2, length, sub, HD), BF16),
        [SSPEC] * 2 + [VSPEC] * 10,
        [
            pltpu.VMEM((length + keep, sub, HD), F32),
            pltpu.VMEM((2, length, sub, HD), F32),
            pltpu.VMEM((2, length, sub, HD), F32),
            pltpu.VMEM((2, length, sub, HD), F32),
            pltpu.VMEM((state, sub, HD), F32),
        ],
        pl.CostEstimate(flops=2 * length * inner * state * 6, bytes_accessed=4 << 20, transcendentals=2 * length * inner * state),
    )(
        readers,
        bc,
        state0.reshape(rows, sub, HD),
        state1.reshape(rows, sub, HD),
        x_t,
        dt_t,
        z_t,
        tiled(dt_bias),
        tiled(a_log),
        tiled(bypass_gain),
        tiled(conv_w),
        tiled(conv_b),
    )
    mamba_out = scan_out.reshape(1, 2, length, inner)

    attention_out = call(
        functools.partial(join_body, heads, spans),
        jax.ShapeDtypeStruct((2, length, heads * Q_PER_KV * HD), BF16),
        [SSPEC] + [VSPEC] * (2 + (1 + heads) * spans),
        (),
        pl.CostEstimate(flops=1 << 24, bytes_accessed=2 << 20, transcendentals=1 << 16),
    )(readers, message, new_kv[0], *got0, *got1)[None]
    return (attention_out, mamba_out)


def solution(mesh):
    row = ("groups", "replica")
    placed = (
        P(row, None, None, "channel"),
        P(row, None, None, "channel"),
        P(row, None, "channel"),
        P(row, None, "channel"),
        P(row, None, "channel"),
        P(row, None, None, "channel"),
        P(row, None, "channel"),
        P(row, None, "channel"),
        P("groups"),
        P(row),
        P("groups", None),
        P("groups", None),
        P("groups"),
        P(row),
        P(row, None, None, "channel"),
        P(row, None, None, "channel"),
        P(row, None, None, "channel"),
        P("channel"),
        P(None, "channel"),
        P("channel"),
        P(None, "channel"),
        P("channel"),
        P("channel", None),
    )
    return jax.shard_map(
        functools.partial(local, mesh.shape["replica"]),
        mesh=mesh,
        in_specs=placed,
        out_specs=(P(row, None, None, "channel"), P(row, None, None, "channel")),
        check_vma=False,
    )
```

```python
import functools
import math

import jax
import jax.numpy as jnp
from jax import lax
from jax.experimental import pallas as pl
from jax.experimental.pallas import tpu as pltpu
from jax.sharding import PartitionSpec as P

HD = 128
Q_PER_KV = 8
F32 = jnp.float32
BF16 = jnp.bfloat16
LOG2E = math.log2(math.e)
SCORE2 = HD ** (-0.5) * LOG2E
LOW = -1e30
STAT = 16
VMEM_LIMIT = 48 * 1024 * 1024

VSPEC = pl.BlockSpec(memory_space=pltpu.VMEM)
SSPEC = pl.BlockSpec(memory_space=pltpu.SMEM)


def call(body, out_shape, specs, scratch=(), cost=None):
    return pl.pallas_call(
        body,
        out_shape=out_shape,
        in_specs=specs,
        out_specs=jax.tree.map(lambda _: VSPEC, out_shape),
        scratch_shapes=list(scratch),
        compiler_params=pltpu.CompilerParams(vmem_limit_bytes=VMEM_LIMIT),
        cost_estimate=cost,
    )


def dot(a, b, ca, cb):
    return lax.dot_general(a, b, (((ca,), (cb,)), ((), ())), preferred_element_type=F32)


def pieces(row, count):
    out = []
    for _ in range(count):
        part = row.astype(BF16).astype(F32)
        out.append(part)
        row = row - part
    return out


def stat_block(rows, width):
    index = lax.broadcasted_iota(jnp.int32, (STAT, width), 0)
    block = jnp.zeros((STAT, width), F32)
    for i, row in enumerate(rows):
        block = jnp.where(index == i, row, block)
    return block.astype(BF16)


def stats_of(part_ref, base, head):
    block = part_ref[base : base + STAT, :].astype(F32)
    o = 5 * head
    top = block[o : o + 1] + block[o + 1 : o + 2] + block[o + 2 : o + 3]
    total = block[o + 3 : o + 4] + block[o + 4 : o + 5]
    return top, total


def folded_softmax(done, kv, at, q):
    step = math.gcd(kv.shape[0], HD)
    parts = list(done)
    for c in range(0, kv.shape[0], step):
        s = dot(kv[c : c + step, at : at + HD], q, 1, 1)
        high = jnp.max(s, axis=0, keepdims=True)
        p = jnp.exp2((s - high) * SCORE2)
        value = dot(kv[c : c + step, at + HD : at + 2 * HD], p.astype(BF16), 0, 0)
        parts.append((high, jnp.sum(p, axis=0, keepdims=True), value))
    m = functools.reduce(jnp.maximum, [part[0] for part in parts])
    fades = [jnp.exp2((part[0] - m) * SCORE2) for part in parts]
    l = sum(f * part[1] for f, part in zip(fades, parts))
    o = sum(f * part[2] for f, part in zip(fades, parts))
    return m, l, o


def prefix_body(heads, spans, pair, *refs):
    me, owner, own, nbr = refs[:4]
    qs = refs[4 : 4 + spans]
    outs = refs[4 + spans : 4 + 2 * spans]
    kv = refs[4 + 2 * spans]
    here = owner[0] // pair == me[0] // pair
    rows = heads * HD

    @pl.when(here)
    def _():
        kv[...] = jnp.where(owner[0] == me[0], own[...], nbr[...])
        for q, out in zip(qs, outs):
            wide = Q_PER_KV * (q.shape[0] - STAT) // (2 * heads * Q_PER_KV)
            stats = []
            for h in range(heads):
                qh = q[h * wide : (h + 1) * wide, :]
                m, l, o = folded_softmax([], kv, 2 * h * HD, qh)
                out[h * HD : (h + 1) * HD, :] = o.astype(BF16)
                stats += pieces(m, 3) + pieces(l, 2)
            out[rows:, :] = stat_block(stats, wide)

    @pl.when(jnp.logical_not(here))
    def _():
        for q, out in zip(qs, outs):
            wide = out.shape[1]
            out[:rows, :] = jnp.zeros((rows, wide), BF16)
            low = jnp.full((1, wide), LOW, F32)
            zero = jnp.zeros((1, wide), F32)
            out[rows:, :] = stat_block((pieces(low, 3) + [zero, zero]) * heads, wide)


def blocks_body(heads, spans, slots, pair, *refs):
    me, src, blk, own, nbr = refs[:5]
    qs = refs[5 : 5 + spans]
    outs = refs[5 + spans : 5 + 2 * spans]
    acc, top, tot = refs[5 + 2 * spans :]
    z, y = me[0] // pair, lax.rem(me[0], pair)
    rows = heads * HD
    full = qs[0].shape[0] - STAT
    wide = outs[0].shape[1]
    ctxs = [jnp.max(q[full:, :].astype(F32)) for q in qs]
    for k, (q, out, ctx) in enumerate(zip(qs, outs, ctxs)):
        reader = lax.rem(z + (spans - k), spans) * pair + y
        acc[...] = jnp.zeros_like(acc)
        top[...] = jnp.full(top.shape, LOW, F32)
        tot[...] = jnp.zeros_like(tot)

        def slot(j, carry, q=q, reader=reader, ctx=ctx):
            source = src[reader, j]
            live = (source // pair == z) & (j.astype(F32) < ctx)

            @pl.when(live)
            def _():
                b = blk[reader, j]
                mine = lax.rem(source, pair) == y
                for h in range(heads):
                    at = slice(2 * h * HD, 2 * (h + 1) * HD)
                    kv = jnp.where(mine, own[b, :, at], nbr[b, :, at])
                    lo = full // 2 + h * wide
                    done = [(top[h], tot[h], acc[h])]
                    top[h], tot[h], acc[h] = folded_softmax(done, kv, 0, q[lo : lo + wide, :])

            return carry

        lax.fori_loop(0, slots, slot, 0)
        stats = []
        for h in range(heads):
            out[h * HD : (h + 1) * HD, :] = acc[h].astype(BF16)
            stats += pieces(top[h], 3) + pieces(tot[h], 2)
        out[rows:, :] = stat_block(stats, wide)


def join_body(heads, spans, *refs):
    flag, q, new = refs[:3]
    parts = [refs[3 : 3 + spans], refs[3 + spans : 3 + 2 * spans]]
    out = refs[3 + 2 * spans]
    fresh = new.shape[1]
    half = q.shape[0] - STAT
    wide = half // (2 * heads)
    rows = heads * HD
    for r in range(2):
        for h in range(heads):
            lo = r * half // 2 + h * wide
            s = dot(new[r, :, 2 * h * HD : (2 * h + 1) * HD], q[lo : lo + wide, :], 1, 1)
            key = lax.broadcasted_iota(jnp.int32, (fresh, wide), 0)
            token = lax.rem(lax.broadcasted_iota(jnp.int32, (fresh, wide), 1), fresh)
            seen = key <= token
            s = jnp.where(seen, s, LOW)
            best = jnp.max(s, axis=0, keepdims=True)
            at = h * HD
            stats = [stats_of(part, rows, h) for part in parts[r]]
            if r == 0:
                stats = [(jnp.where(flag[0] > 0, m, LOW), l) for m, l in stats]
            for m, _ in stats:
                best = jnp.maximum(best, m)
            p = jnp.where(seen, jnp.exp2((s - best) * SCORE2), 0.0)
            total = jnp.sum(p, axis=0, keepdims=True)
            o = dot(new[r, :, (2 * h + 1) * HD : (2 * h + 2) * HD], p.astype(BF16), 0, 0)
            for part, (m, l) in zip(parts[r], stats):
                w = jnp.exp2((m - best) * SCORE2)
                total = total + w * l
                o = o + w * part[at : at + HD, :].astype(F32)
            done = jnp.transpose(o / total).astype(BF16)
            for g in range(Q_PER_KV):
                col = (h * Q_PER_KV + g) * HD
                out[r, :, col : col + HD] = done[g * fresh : (g + 1) * fresh, :]


def reach(away, spans, rounds, here):
    low = high = away
    for r in range(rounds):
        odd = r % 2
        below = jnp.where((lax.rem(low, 2) != odd) & (low > 0), low - 1, low)
        above = jnp.where((lax.rem(high, 2) == odd) & (high < spans - 1), high + 1, high)
        low, high = below, above
    return (low <= here) & (here <= high)


def shared_body(spans, pair, unit, rounds, me, owner, kept, came, out):
    z, y = me[0] // pair, lax.rem(me[0], pair)
    if rounds == 0:
        take = lax.rem(owner[0], pair) != y
        base = unit
    else:
        away = owner[0] // pair
        take = jnp.logical_not(reach(away, spans, rounds - 1, z))
        base = 0
    out[...] = jnp.where(take, came[base:, :], kept[base:, :])


def state_send_body(spans, pair, unit, me, src, own, nbr, *outs):
    z, y = me[0] // pair, lax.rem(me[0], pair)
    for k, out in enumerate(outs):
        source = src[lax.rem(z + k, spans) * pair + y]
        out[...] = jnp.where(lax.rem(source, pair) == y, own[:unit, :], nbr[:unit, :])


def state_take_body(spans, pair, me, src, *refs):
    came, out = refs[:spans], refs[spans]
    z = me[0] // pair
    k1 = lax.rem(z + spans - src[me[0]] // pair, spans)
    for k in range(spans):

        @pl.when(k1 == k)
        def _(k=k):
            out[...] = came[k][...]


def silu(x):
    return x / (1.0 + jnp.exp(-x))


def gains_body(chunk, flag, st0, st1, x, w, b, wbc, out, pad):
    taps = w.shape[0]
    keep = taps - 1
    length = x.shape[1]
    lead = 8
    total = [jnp.zeros((length, wbc.shape[0]), F32) for _ in range(2)]
    for c in range(0, x.shape[2], chunk):
        at = slice(c, c + chunk)
        for r, st in enumerate((st0, st1)):
            first = st[:, at].astype(F32)
            if r == 0:
                first = jnp.where(flag[0] > 0, first, 0.0)
            pad[r, lead - keep : lead, :] = first
            pad[r, lead:, :] = x[r, :, at].astype(F32)
            acc = b[:, at] + w[0:1, at] * pad[r, lead - keep : lead - keep + length, :]
            for k in range(1, taps):
                acc = acc + w[k : k + 1, at] * pad[r, lead - keep + k : lead - keep + k + length, :]
            total[r] = total[r] + dot(silu(acc).astype(BF16), wbc[:, at], 1, 1)
    for r in range(2):
        out[r] = total[r]


def scan_body(state, flag, bc, st0, st1, x, dt, zg, dtb, alog, gain, w, b, out, pad, step, push, res, dec):
    taps = w.shape[0]
    keep = taps - 1
    length = x.shape[1]
    sub = x.shape[2]
    block = 16
    dec[...] = jnp.exp(alog[...]) * (-LOG2E)
    for r, st in enumerate((st0, st1)):
        first = st[state : state + keep].astype(F32)
        if r == 0:
            first = jnp.where(flag[0] > 0, first, 0.0)
        pad[0:keep] = first
        pad[keep:] = x[r].astype(F32)

        def prepare(t, carry, r=r):
            acc = b[...] + w[0] * pad[t]
            for k in range(1, taps):
                acc = acc + w[k] * pad[t + k]
            sig = silu(acc)
            raw = dt[r, t].astype(F32) + dtb[...]
            now = jnp.maximum(raw, 0.0) + jnp.log1p(jnp.exp(-jnp.abs(raw)))
            step[r, t] = now
            push[r, t] = now * sig
            res[r, t] = gain[...] * sig
            return carry

        lax.fori_loop(0, length, prepare, 0, unroll=4)

    for r, st in enumerate((st0, st1)):
        for c in range(0, sub, block):
            at = slice(c, c + block)
            start = []
            for n in range(state):
                h = st[n, at, :].astype(F32)
                if r == 0:
                    h = jnp.where(flag[0] > 0, h, 0.0)
                start.append(h)

            def advance(t, hs, r=r, at=at):
                now = step[r, t, at, :]
                add = push[r, t, at, :]
                sums = [res[r, t, at, :], None, None, None]
                after = []
                for n in range(state):
                    h = jnp.exp2(now * dec[n, at, :]) * hs[n] + bc[r * length + t, n] * add
                    term = bc[r * length + t, state + n] * h
                    i = n % 4
                    sums[i] = term if sums[i] is None else sums[i] + term
                    after.append(h)
                y = (sums[0] + sums[1]) + (sums[2] + sums[3])
                gate = silu(zg[r, t, at, :].astype(F32))
                out[r, t, at, :] = (y * gate).astype(BF16)
                return tuple(after)

            lax.fori_loop(0, length, advance, tuple(start), unroll=2)


def local(
    size,
    queries,
    new_kv,
    cached_lookup_pairs,
    prefix_ssm,
    prefix_conv,
    pool_kv,
    pool_ssm,
    pool_conv,
    owner_id,
    readers,
    restore_src,
    restore_blk,
    state_src,
    ctx_blocks,
    mamba_x,
    mamba_z,
    mamba_dt,
    dt_bias,
    a_log,
    bypass_gain,
    conv_w,
    conv_b,
    w_bc,
):
    axis = "replica"
    pair = 2
    spans = size // pair
    length = queries.shape[2]
    heads = new_kv.shape[3] // (2 * HD)
    wide = Q_PER_KV * length
    slots = restore_src.shape[1]
    inner = mamba_x.shape[3]
    state = a_log.shape[0]
    keep = prefix_conv.shape[1]
    me = lax.axis_index(axis)[None]

    def across(value):
        return lax.ppermute(value, axis, [(s, s ^ 1) for s in range(size)])

    def turn(value, k):
        return lax.ppermute(value, axis, [(s, (s + k * pair) % size) for s in range(size)])

    def after(value, *others):
        return lax.optimization_barrier((value, *others))[0]

    sub = inner // HD

    def tiled(value):
        return value.reshape(value.shape[:-1] + (sub, HD))

    cols = 2 * HD
    rows = state + keep
    unit = rows * inner // cols
    states = jnp.concatenate([pool_ssm[0], pool_conv[0], prefix_ssm[0], prefix_conv[0]], axis=0)
    states = states.reshape(2 * unit, cols)
    states_nbr = across(states)

    folded = queries[0].reshape(2, length, heads * Q_PER_KV, HD).transpose(0, 2, 1, 3)
    folded = folded.reshape(2 * heads * wide, HD)
    length_rows = jnp.full((STAT, HD), ctx_blocks[0].astype(BF16), BF16)
    message = jnp.concatenate([folded, length_rows], axis=0)
    asked = [message] + [turn(message, k) for k in range(1, spans)]

    x_t, dt_t, z_t = tiled(mamba_x[0]), tiled(mamba_dt[0]), tiled(mamba_z[0])
    prefix_nbr = across(cached_lookup_pairs[0])

    one = jax.ShapeDtypeStruct((unit, cols), BF16)

    def shared(rounds, kept, came):
        return call(
            functools.partial(shared_body, spans, pair, unit, rounds),
            one,
            [SSPEC] * 2 + [VSPEC] * 2,
        )(me, owner_id, kept, came)

    def hop(value, r):
        odd = r % 2
        near = [(i, i + 1) for i in range(odd, spans - 1, 2)]
        links = [(pair * u + j, pair * v + j) for i, n in near for u, v in ((i, n), (n, i)) for j in range(pair)]
        return lax.ppermute(value, axis, links)

    state0 = shared(0, states, states_nbr)
    hops = [hop(state0, 0)] if spans > 1 else []

    sent = call(
        functools.partial(state_send_body, spans, pair, unit),
        [one] * spans,
        [SSPEC] * 2 + [VSPEC] * 2,
        (),
        pl.CostEstimate(flops=50 * 10**9, bytes_accessed=150 * 10**6, transcendentals=0),
    )(after(me, x_t, dt_t, z_t, *asked[1:], *hops[:1]), state_src, states, states_nbr)
    came = [sent[0]] + [turn(sent[k], k) for k in range(1, spans)]
    state1 = call(
        functools.partial(state_take_body, spans, pair),
        one,
        [SSPEC] * 2 + [VSPEC] * spans,
    )(me, state_src, *came)
    part_shape = jax.ShapeDtypeStruct((heads * HD + STAT, wide), BF16)
    keys = cached_lookup_pairs.shape[1]
    part0 = call(
        functools.partial(prefix_body, heads, spans, pair),
        [part_shape] * spans,
        [SSPEC] * 2 + [VSPEC] * (2 + spans),
        [pltpu.VMEM(cached_lookup_pairs.shape[1:], BF16)],
        pl.CostEstimate(flops=50 * 10**9, bytes_accessed=150 * 10**6, transcendentals=0),
    )(me, owner_id, cached_lookup_pairs[0], prefix_nbr, *asked)
    for r in range(1, spans):
        state0 = shared(r, state0, hops[-1])
        if r < spans - 1:
            hops.append(hop(after(state0, sent[0]), r))
    got0 = [part0[0]] + [turn(after(part0[k], came[spans - k]), spans - k) for k in range(1, spans)]

    pool_nbr = across(after(pool_kv[0], sent[0]))
    part1 = call(
        functools.partial(blocks_body, heads, spans, slots, pair),
        [part_shape] * spans,
        [SSPEC] * 3 + [VSPEC] * (2 + spans),
        [pltpu.VMEM((heads, HD, wide), F32), pltpu.VMEM((heads, 1, wide), F32), pltpu.VMEM((heads, 1, wide), F32)],
        pl.CostEstimate(flops=20 * 10**9, bytes_accessed=60 * 10**6, transcendentals=0),
    )(after(me, *got0[1:]), restore_src, restore_blk, pool_kv[0], pool_nbr, *asked)
    got1 = [part1[0]] + [turn(part1[k], spans - k) for k in range(1, spans)]

    first = state * inner // cols

    def taps_of(value):
        return value[first:].reshape(keep, inner)

    chunk = math.gcd(inner, 512)
    partial = call(
        functools.partial(gains_body, chunk),
        jax.ShapeDtypeStruct((2, length, w_bc.shape[1]), F32),
        [SSPEC] + [VSPEC] * 6,
        [pltpu.VMEM((2, length + 8, chunk), F32)],
        pl.CostEstimate(flops=2 * 2 * length * inner * 32, bytes_accessed=2 << 20, transcendentals=2 * length * inner),
    )(readers, taps_of(state0), taps_of(state1), mamba_x[0], conv_w, conv_b[None], w_bc.T)
    both = partial + lax.ppermute(partial, "channel", [(0, 1), (1, 0)])
    bc = both.reshape(2 * length, w_bc.shape[1])
    scan_out = call(
        functools.partial(scan_body, state),
        jax.ShapeDtypeStruct((2, length, sub, HD), BF16),
        [SSPEC] * 2 + [VSPEC] * 10,
        [
            pltpu.VMEM((length + keep, sub, HD), F32),
            pltpu.VMEM((2, length, sub, HD), F32),
            pltpu.VMEM((2, length, sub, HD), F32),
            pltpu.VMEM((2, length, sub, HD), F32),
            pltpu.VMEM((state, sub, HD), F32),
        ],
        pl.CostEstimate(flops=2 * length * inner * state * 6, bytes_accessed=4 << 20, transcendentals=2 * length * inner * state),
    )(
        readers,
        bc,
        state0.reshape(rows, sub, HD),
        state1.reshape(rows, sub, HD),
        x_t,
        dt_t,
        z_t,
        tiled(dt_bias),
        tiled(a_log),
        tiled(bypass_gain),
        tiled(conv_w),
        tiled(conv_b),
    )
    mamba_out = scan_out.reshape(1, 2, length, inner)

    attention_out = call(
        functools.partial(join_body, heads, spans),
        jax.ShapeDtypeStruct((2, length, heads * Q_PER_KV * HD), BF16),
        [SSPEC] + [VSPEC] * (2 + 2 * spans),
        (),
        pl.CostEstimate(flops=1 << 24, bytes_accessed=2 << 20, transcendentals=1 << 16),
    )(readers, message, new_kv[0], *got0, *got1)[None]
    return (attention_out, mamba_out)


def solution(mesh):
    row = ("groups", "replica")
    placed = (
        P(row, None, None, "channel"),
        P(row, None, None, "channel"),
        P(row, None, "channel"),
        P(row, None, "channel"),
        P(row, None, "channel"),
        P(row, None, None, "channel"),
        P(row, None, "channel"),
        P(row, None, "channel"),
        P("groups"),
        P(row),
        P("groups", None),
        P("groups", None),
        P("groups"),
        P(row),
        P(row, None, None, "channel"),
        P(row, None, None, "channel"),
        P(row, None, None, "channel"),
        P("channel"),
        P(None, "channel"),
        P("channel"),
        P(None, "channel"),
        P("channel"),
        P("channel", None),
    )
    return jax.shard_map(
        functools.partial(local, mesh.shape["replica"]),
        mesh=mesh,
        in_specs=placed,
        out_specs=(P(row, None, None, "channel"), P(row, None, None, "channel")),
        check_vma=False,
    )
```

```python
import functools
import math

import jax
import jax.numpy as jnp
from jax import lax
from jax.experimental import pallas as pl
from jax.experimental.pallas import tpu as pltpu
from jax.sharding import PartitionSpec as P

HD = 128
Q_PER_KV = 8
F32 = jnp.float32
BF16 = jnp.bfloat16
LOG2E = math.log2(math.e)
SCORE2 = HD ** (-0.5) * LOG2E
LOW = -1e30
STAT = 16
VMEM_LIMIT = 48 * 1024 * 1024

VSPEC = pl.BlockSpec(memory_space=pltpu.VMEM)
SSPEC = pl.BlockSpec(memory_space=pltpu.SMEM)


def call(body, out_shape, specs, scratch=(), cost=None):
    return pl.pallas_call(
        body,
        out_shape=out_shape,
        in_specs=specs,
        out_specs=jax.tree.map(lambda _: VSPEC, out_shape),
        scratch_shapes=list(scratch),
        compiler_params=pltpu.CompilerParams(vmem_limit_bytes=VMEM_LIMIT),
        cost_estimate=cost,
    )


def dot(a, b, ca, cb):
    return lax.dot_general(a, b, (((ca,), (cb,)), ((), ())), preferred_element_type=F32)


def pieces(row, count):
    out = []
    for _ in range(count):
        part = row.astype(BF16).astype(F32)
        out.append(part)
        row = row - part
    return out


def stat_block(rows, width):
    index = lax.broadcasted_iota(jnp.int32, (STAT, width), 0)
    block = jnp.zeros((STAT, width), F32)
    for i, row in enumerate(rows):
        block = jnp.where(index == i, row, block)
    return block.astype(BF16)


def stats_of(part_ref, base, head):
    block = part_ref[base : base + STAT, :].astype(F32)
    o = 5 * head
    top = block[o : o + 1] + block[o + 1 : o + 2] + block[o + 2 : o + 3]
    total = block[o + 3 : o + 4] + block[o + 4 : o + 5]
    return top, total


def folded_softmax(done, kv, at, q):
    step = math.gcd(kv.shape[0], HD)
    parts = list(done)
    for c in range(0, kv.shape[0], step):
        s = dot(kv[c : c + step, at : at + HD], q, 1, 1)
        high = jnp.max(s, axis=0, keepdims=True)
        p = jnp.exp2((s - high) * SCORE2)
        value = dot(kv[c : c + step, at + HD : at + 2 * HD], p.astype(BF16), 0, 0)
        parts.append((high, jnp.sum(p, axis=0, keepdims=True), value))
    m = functools.reduce(jnp.maximum, [part[0] for part in parts])
    fades = [jnp.exp2((part[0] - m) * SCORE2) for part in parts]
    l = sum(f * part[1] for f, part in zip(fades, parts))
    o = sum(f * part[2] for f, part in zip(fades, parts))
    return m, l, o


def prefix_body(heads, spans, pair, *refs):
    me, owner, own, nbr = refs[:4]
    qs = refs[4 : 4 + spans]
    outs = refs[4 + spans : 4 + 2 * spans]
    kv = refs[4 + 2 * spans]
    here = owner[0] // pair == me[0] // pair
    rows = heads * HD

    @pl.when(here)
    def _():
        kv[...] = jnp.where(owner[0] == me[0], own[...], nbr[...])
        for q, out in zip(qs, outs):
            wide = Q_PER_KV * (q.shape[0] - STAT) // (2 * heads * Q_PER_KV)
            stats = []
            for h in range(heads):
                qh = q[h * wide : (h + 1) * wide, :]
                m, l, o = folded_softmax([], kv, 2 * h * HD, qh)
                out[h * HD : (h + 1) * HD, :] = o.astype(BF16)
                stats += pieces(m, 3) + pieces(l, 2)
            out[rows:, :] = stat_block(stats, wide)

    @pl.when(jnp.logical_not(here))
    def _():
        for q, out in zip(qs, outs):
            wide = out.shape[1]
            out[:rows, :] = jnp.zeros((rows, wide), BF16)
            low = jnp.full((1, wide), LOW, F32)
            zero = jnp.zeros((1, wide), F32)
            out[rows:, :] = stat_block((pieces(low, 3) + [zero, zero]) * heads, wide)


def blocks_body(last, heads, spans, slots, pair, *refs):
    me, src, blk, pool = refs[:4]
    qs = refs[4 : 4 + spans]
    refs = refs[4 + spans :]
    if last:
        before, outs, (top, tot, acc) = refs[:3], refs[3 : 3 + spans], refs[3 + spans :]
    else:
        top, tot, acc = refs
    z = me[0] // pair
    rows = heads * HD
    full = qs[0].shape[0] - STAT
    wide = acc.shape[-1]
    ctxs = [jnp.max(q[full:, :].astype(F32)) for q in qs]
    if last:
        for ref, old in zip((top, tot, acc), before):
            ref[...] = old[...]
    else:
        top[...] = jnp.full(top.shape, LOW, F32)
        tot[...] = jnp.zeros_like(tot)
        acc[...] = jnp.zeros_like(acc)
    for k, (q, ctx) in enumerate(zip(qs, ctxs)):
        reader = lax.rem(z + (spans - k), spans) * pair + lax.rem(me[0], pair)

        def slot(j, carry, k=k, q=q, reader=reader, ctx=ctx):
            source = src[reader, j]
            held = (source // pair == z) & (source != me[0]) if last else source == me[0]

            @pl.when(held & (j.astype(F32) < ctx))
            def _():
                b = blk[reader, j]
                for h in range(heads):
                    kv = pool[b, :, 2 * h * HD : 2 * (h + 1) * HD]
                    lo = full // 2 + h * wide
                    done = [(top[k, h], tot[k, h], acc[k, h])]
                    top[k, h], tot[k, h], acc[k, h] = folded_softmax(done, kv, 0, q[lo : lo + wide, :])

            return carry

        lax.fori_loop(0, slots, slot, 0)
    if last:
        for k, out in enumerate(outs):
            stats = []
            for h in range(heads):
                out[h * HD : (h + 1) * HD, :] = acc[k, h].astype(BF16)
                stats += pieces(top[k, h], 3) + pieces(tot[k, h], 2)
            out[rows:, :] = stat_block(stats, wide)


def fresh_softmax(new, r, h, q):
    fresh, wide = new.shape[1], q.shape[0]
    s = dot(new[r, :, 2 * h * HD : (2 * h + 1) * HD], q, 1, 1)
    key = lax.broadcasted_iota(jnp.int32, (fresh, wide), 0)
    token = lax.rem(lax.broadcasted_iota(jnp.int32, (fresh, wide), 1), fresh)
    seen = key <= token
    m = jnp.max(jnp.where(seen, s, LOW), axis=0, keepdims=True)
    p = jnp.where(seen, jnp.exp2((s - m) * SCORE2), 0.0)
    o = dot(new[r, :, (2 * h + 1) * HD : (2 * h + 2) * HD], p.astype(BF16), 0, 0)
    return m, jnp.sum(p, axis=0, keepdims=True), o


def join(parts):
    m = functools.reduce(jnp.maximum, [part[0] for part in parts])
    fades = [jnp.exp2((part[0] - m) * SCORE2) for part in parts]
    total = sum(f * part[1] for f, part in zip(fades, parts))
    return jnp.transpose(sum(f * part[2] for f, part in zip(fades, parts)) / total).astype(BF16)


def part_of(ref, heads, h):
    m, l = stats_of(ref, heads * HD, h)
    return m, l, ref[h * HD : (h + 1) * HD, :].astype(F32)


def join0_body(heads, spans, flag, q, new, *refs):
    parts, (out, top, tot, acc) = refs[:spans], refs[spans:]
    fresh = new.shape[1]
    wide = acc.shape[-1]
    half = heads * wide
    for h in range(heads):
        found = [fresh_softmax(new, 0, h, q[h * wide : (h + 1) * wide, :])]
        for part in parts:
            m, l, o = part_of(part, heads, h)
            found.append((jnp.where(flag[0] > 0, m, LOW), l, o))
        done = join(found)
        for g in range(Q_PER_KV):
            col = (h * Q_PER_KV + g) * HD
            out[:, col : col + HD] = done[g * fresh : (g + 1) * fresh, :]
        top[h], tot[h], acc[h] = fresh_softmax(new, 1, h, q[half + h * wide : half + (h + 1) * wide, :])


def join1_body(heads, spans, first, top, tot, acc, *refs):
    parts, out = refs[:spans], refs[spans]
    fresh = first.shape[0]
    out[0] = first[...]
    for h in range(heads):
        done = join([(top[h], tot[h], acc[h])] + [part_of(part, heads, h) for part in parts])
        for g in range(Q_PER_KV):
            col = (h * Q_PER_KV + g) * HD
            out[1, :, col : col + HD] = done[g * fresh : (g + 1) * fresh, :]


def reach(away, spans, rounds, here):
    low = high = away
    for r in range(rounds):
        odd = r % 2
        below = jnp.where((lax.rem(low, 2) != odd) & (low > 0), low - 1, low)
        above = jnp.where((lax.rem(high, 2) == odd) & (high < spans - 1), high + 1, high)
        low, high = below, above
    return (low <= here) & (here <= high)


def shared_body(spans, pair, unit, rounds, me, owner, kept, came, out):
    z, y = me[0] // pair, lax.rem(me[0], pair)
    if rounds == 0:
        take = lax.rem(owner[0], pair) != y
        base = unit
    else:
        away = owner[0] // pair
        take = jnp.logical_not(reach(away, spans, rounds - 1, z))
        base = 0
    out[...] = jnp.where(take, came[base:, :], kept[base:, :])


def state_send_body(spans, pair, unit, me, src, own, nbr, *outs):
    z, y = me[0] // pair, lax.rem(me[0], pair)
    for k, out in enumerate(outs):
        source = src[lax.rem(z + k, spans) * pair + y]
        out[...] = jnp.where(lax.rem(source, pair) == y, own[:unit, :], nbr[:unit, :])


def state_take_body(spans, pair, me, src, *refs):
    came, out = refs[:spans], refs[spans]
    z = me[0] // pair
    k1 = lax.rem(z + spans - src[me[0]] // pair, spans)
    for k in range(spans):

        @pl.when(k1 == k)
        def _(k=k):
            out[...] = came[k][...]


def silu(x):
    return x / (1.0 + jnp.exp(-x))


def gains_body(chunk, flag, st0, st1, x, w, b, wbc, out, pad):
    taps = w.shape[0]
    keep = taps - 1
    length = x.shape[1]
    lead = 8
    total = [jnp.zeros((length, wbc.shape[0]), F32) for _ in range(2)]
    for c in range(0, x.shape[2], chunk):
        at = slice(c, c + chunk)
        for r, st in enumerate((st0, st1)):
            first = st[:, at].astype(F32)
            if r == 0:
                first = jnp.where(flag[0] > 0, first, 0.0)
            pad[r, lead - keep : lead, :] = first
            pad[r, lead:, :] = x[r, :, at].astype(F32)
            acc = b[:, at] + w[0:1, at] * pad[r, lead - keep : lead - keep + length, :]
            for k in range(1, taps):
                acc = acc + w[k : k + 1, at] * pad[r, lead - keep + k : lead - keep + k + length, :]
            total[r] = total[r] + dot(silu(acc).astype(BF16), wbc[:, at], 1, 1)
    for r in range(2):
        out[r] = total[r]


def ready_body(x, dt, zg, dtb, alog, w, b, step, act, gate, dec):
    taps, length = w.shape[0], x.shape[1]
    dec[...] = jnp.exp(alog[...]) * (-LOG2E)
    for r in range(2):

        def basics(t, carry, r=r):
            raw = dt[r, t].astype(F32) + dtb[...]
            step[r, t] = jnp.maximum(raw, 0.0) + jnp.log1p(jnp.exp(-jnp.abs(raw)))
            gate[r, t] = silu(zg[r, t].astype(F32))
            return carry

        lax.fori_loop(0, length, basics, 0, unroll=4)

        def total(t, first, r=r):
            acc = b[...]
            for k in range(first, taps):
                acc = acc + w[k] * x[r, t + k - taps + 1].astype(F32)
            return acc

        for t in range(taps - 1):
            act[r, t] = total(t, taps - 1 - t)

        def later(t, carry, r=r):
            act[r, t] = silu(total(t, 0))
            return carry

        lax.fori_loop(taps - 1, length, later, 0)


def scan_body(state, flag, bc, st0, st1, step, act, gate, dec, gain, w, out):
    keep = w.shape[0] - 1
    length, sub = step.shape[1], step.shape[2]
    block = 16
    for r, st in enumerate((st0, st1)):
        for c in range(0, sub, block):
            at = slice(c, c + block)

            def held(n, r=r, st=st, at=at):
                value = st[n, at, :].astype(F32)
                return jnp.where(flag[0] > 0, value, 0.0) if r == 0 else value

            def advance(t, hs, sig, r=r, at=at):
                now = step[r, t, at, :]
                add = now * sig
                sums = [gain[at, :] * sig, None, None, None]
                after = []
                for n in range(state):
                    h = jnp.exp2(now * dec[n, at, :]) * hs[n] + bc[r * length + t, n] * add
                    term = bc[r * length + t, state + n] * h
                    i = n % 4
                    sums[i] = term if sums[i] is None else sums[i] + term
                    after.append(h)
                y = (sums[0] + sums[1]) + (sums[2] + sums[3])
                out[r, t, at, :] = (y * gate[r, t, at, :]).astype(BF16)
                return tuple(after)

            hs = tuple(held(n) for n in range(state))
            peel = keep + (length - keep) % 2
            for t in range(peel):
                sig = act[r, t, at, :]
                if t < keep:
                    for k in range(keep - t):
                        sig = sig + w[k, at, :] * held(state + t + k)
                    sig = silu(sig)
                hs = advance(t, hs, sig)

            def body(t, hs, r=r, at=at, advance=advance):
                return advance(t, hs, act[r, t, at, :])

            lax.fori_loop(peel, length, body, hs, unroll=2)


def local(
    size,
    queries,
    new_kv,
    cached_lookup_pairs,
    prefix_ssm,
    prefix_conv,
    pool_kv,
    pool_ssm,
    pool_conv,
    owner_id,
    readers,
    restore_src,
    restore_blk,
    state_src,
    ctx_blocks,
    mamba_x,
    mamba_z,
    mamba_dt,
    dt_bias,
    a_log,
    bypass_gain,
    conv_w,
    conv_b,
    w_bc,
):
    axis = "replica"
    pair = 2
    spans = size // pair
    length = queries.shape[2]
    heads = new_kv.shape[3] // (2 * HD)
    wide = Q_PER_KV * length
    slots = restore_src.shape[1]
    inner = mamba_x.shape[3]
    state = a_log.shape[0]
    keep = prefix_conv.shape[1]
    me = lax.axis_index(axis)[None]

    def across(value):
        return lax.ppermute(value, axis, [(s, s ^ 1) for s in range(size)])

    def turn(value, k):
        return lax.ppermute(value, axis, [(s, (s + k * pair) % size) for s in range(size)])

    def after(value, *others):
        return lax.optimization_barrier((value, *others))[0]

    sub = inner // HD

    def tiled(value):
        return value.reshape(value.shape[:-1] + (sub, HD))

    cols = 2 * HD
    rows = state + keep
    unit = rows * inner // cols
    states = jnp.concatenate([pool_ssm[0], pool_conv[0], prefix_ssm[0], prefix_conv[0]], axis=0)
    states = states.reshape(2 * unit, cols)
    states_nbr = across(states)

    folded = queries[0].reshape(2, length, heads * Q_PER_KV, HD).transpose(0, 2, 1, 3)
    folded = folded.reshape(2 * heads * wide, HD)
    length_rows = jnp.full((STAT, HD), ctx_blocks[0].astype(BF16), BF16)
    message = jnp.concatenate([folded, length_rows], axis=0)
    asked = [message] + [turn(message, k) for k in range(1, spans)]

    x_t, dt_t, z_t = tiled(mamba_x[0]), tiled(mamba_dt[0]), tiled(mamba_z[0])
    f32_rows = jax.ShapeDtypeStruct((2, length, sub, HD), F32)
    prepared = call(
        ready_body,
        [f32_rows] * 3 + [jax.ShapeDtypeStruct((state, sub, HD), F32)],
        [VSPEC] * 7,
    )(x_t, dt_t, z_t, tiled(dt_bias), tiled(a_log), tiled(conv_w), tiled(conv_b))
    prefix_nbr = across(cached_lookup_pairs[0])

    one = jax.ShapeDtypeStruct((unit, cols), BF16)

    def shared(rounds, kept, came):
        return call(
            functools.partial(shared_body, spans, pair, unit, rounds),
            one,
            [SSPEC] * 2 + [VSPEC] * 2,
            (),
            pl.CostEstimate(flops=50 * 10**9, bytes_accessed=150 * 10**6, transcendentals=0) if rounds == 0 else None,
        )(me, owner_id, kept, came)

    def hop(value, r):
        odd = r % 2
        near = [(i, i + 1) for i in range(odd, spans - 1, 2)]
        links = [(pair * u + j, pair * v + j) for i, n in near for u, v in ((i, n), (n, i)) for j in range(pair)]
        return lax.ppermute(value, axis, links)

    state0 = shared(0, states, states_nbr)
    hops = [hop(state0, 0)] if spans > 1 else []

    sent = call(
        functools.partial(state_send_body, spans, pair, unit),
        [one] * spans,
        [SSPEC] * 2 + [VSPEC] * 2,
        (),
        pl.CostEstimate(flops=50 * 10**9, bytes_accessed=150 * 10**6, transcendentals=0),
    )(after(me, *prepared, *asked[1:], *hops[:1]), state_src, states, states_nbr)
    came = [sent[0]] + [turn(sent[k], k) for k in range(1, spans)]
    state1 = call(
        functools.partial(state_take_body, spans, pair),
        one,
        [SSPEC] * 2 + [VSPEC] * spans,
    )(me, state_src, *came)
    part_shape = jax.ShapeDtypeStruct((heads * HD + STAT, wide), BF16)
    keys = cached_lookup_pairs.shape[1]
    part0 = call(
        functools.partial(prefix_body, heads, spans, pair),
        [part_shape] * spans,
        [SSPEC] * 2 + [VSPEC] * (2 + spans),
        [pltpu.VMEM(cached_lookup_pairs.shape[1:], BF16)],
        pl.CostEstimate(flops=10**6, bytes_accessed=10**4, transcendentals=0),
    )(me, owner_id, cached_lookup_pairs[0], prefix_nbr, *asked)
    for r in range(1, spans):
        state0 = shared(r, after(state0, part0[0]) if r > 1 else state0, hops[-1])
        if r < spans - 1:
            hops.append(hop(after(state0, sent[0]), r))
    got0 = [part0[0]] + [turn(after(part0[k], came[spans - k]), spans - k) for k in range(1, spans)]

    first = state * inner // cols

    def taps_of(value):
        return value[first:].reshape(keep, inner)

    chunk = math.gcd(inner, 512)
    partial = call(
        functools.partial(gains_body, chunk),
        jax.ShapeDtypeStruct((2, length, w_bc.shape[1]), F32),
        [SSPEC] + [VSPEC] * 6,
        [pltpu.VMEM((2, length + 8, chunk), F32)],
        pl.CostEstimate(flops=2 * 2 * length * inner * 32, bytes_accessed=2 << 20, transcendentals=2 * length * inner),
    )(readers, taps_of(state0), taps_of(state1), mamba_x[0], conv_w, conv_b[None], w_bc.T)
    both = partial + lax.ppermute(partial, "channel", [(0, 1), (1, 0)])
    bc = both.reshape(2 * length, w_bc.shape[1])
    pool_nbr = across(pool_kv[0])
    kept = [
        jax.ShapeDtypeStruct((spans, heads, 1, wide), F32),
        jax.ShapeDtypeStruct((spans, heads, 1, wide), F32),
        jax.ShapeDtypeStruct((spans, heads, HD, wide), F32),
    ]
    before = call(
        functools.partial(blocks_body, False, heads, spans, slots, pair),
        kept,
        [SSPEC] * 3 + [VSPEC] * (1 + spans),
    )(after(me, part0[0]), restore_src, restore_blk, pool_kv[0], *asked)
    fresh_shape = jax.ShapeDtypeStruct((length, heads * Q_PER_KV * HD), BF16)
    joined = call(
        functools.partial(join0_body, heads, spans),
        [fresh_shape] + [jax.ShapeDtypeStruct(v.shape[1:], F32) for v in kept],
        [SSPEC] + [VSPEC] * (2 + spans),
    )(readers, message, new_kv[0], *got0)
    part1 = call(
        functools.partial(blocks_body, True, heads, spans, slots, pair),
        [part_shape] * spans,
        [SSPEC] * 3 + [VSPEC] * (4 + spans),
        [pltpu.VMEM(v.shape, F32) for v in kept],
        pl.CostEstimate(flops=20 * 10**9, bytes_accessed=60 * 10**6, transcendentals=0),
    )(after(me, bc, *got0[1:]), restore_src, restore_blk, pool_nbr, *asked, *before)
    got1 = [part1[0]] + [turn(part1[k], spans - k) for k in range(1, spans)]

    scan_out = call(
        functools.partial(scan_body, state),
        jax.ShapeDtypeStruct((2, length, sub, HD), BF16),
        [SSPEC] * 2 + [VSPEC] * 8,
        (),
        pl.CostEstimate(flops=2 * length * inner * state * 6, bytes_accessed=4 << 20, transcendentals=2 * length * inner * state),
    )(readers, bc, state0.reshape(rows, sub, HD), state1.reshape(rows, sub, HD), *prepared, tiled(bypass_gain), tiled(conv_w))
    mamba_out = scan_out.reshape(1, 2, length, inner)

    attention_out = call(
        functools.partial(join1_body, heads, spans),
        jax.ShapeDtypeStruct((2,) + fresh_shape.shape, BF16),
        [VSPEC] * (4 + spans),
    )(*joined, *got1)[None]
    return (attention_out, mamba_out)


def solution(mesh):
    row = ("groups", "replica")
    placed = (
        P(row, None, None, "channel"),
        P(row, None, None, "channel"),
        P(row, None, "channel"),
        P(row, None, "channel"),
        P(row, None, "channel"),
        P(row, None, None, "channel"),
        P(row, None, "channel"),
        P(row, None, "channel"),
        P("groups"),
        P(row),
        P("groups", None),
        P("groups", None),
        P("groups"),
        P(row),
        P(row, None, None, "channel"),
        P(row, None, None, "channel"),
        P(row, None, None, "channel"),
        P("channel"),
        P(None, "channel"),
        P("channel"),
        P(None, "channel"),
        P("channel"),
        P("channel", None),
    )
    return jax.shard_map(
        functools.partial(local, mesh.shape["replica"]),
        mesh=mesh,
        in_specs=placed,
        out_specs=(P(row, None, None, "channel"), P(row, None, None, "channel")),
        check_vma=False,
    )
```

```python
import functools
import math

import jax
import jax.numpy as jnp
from jax import lax
from jax.experimental import pallas as pl
from jax.experimental.pallas import tpu as pltpu
from jax.sharding import PartitionSpec as P

HD = 128
Q_PER_KV = 8
F32 = jnp.float32
BF16 = jnp.bfloat16
LOG2E = math.log2(math.e)
SCORE2 = HD ** (-0.5) * LOG2E
LOW = -1e30
STAT = 16
VMEM_LIMIT = 48 * 1024 * 1024

VSPEC = pl.BlockSpec(memory_space=pltpu.VMEM)
SSPEC = pl.BlockSpec(memory_space=pltpu.SMEM)


def call(body, out_shape, specs, scratch=(), cost=None):
    return pl.pallas_call(
        body,
        out_shape=out_shape,
        in_specs=specs,
        out_specs=jax.tree.map(lambda _: VSPEC, out_shape),
        scratch_shapes=list(scratch),
        compiler_params=pltpu.CompilerParams(vmem_limit_bytes=VMEM_LIMIT),
        cost_estimate=cost,
    )


def dot(a, b, ca, cb):
    return lax.dot_general(a, b, (((ca,), (cb,)), ((), ())), preferred_element_type=F32)


def pieces(row, count):
    out = []
    for _ in range(count):
        part = row.astype(BF16).astype(F32)
        out.append(part)
        row = row - part
    return out


def stat_block(rows, width):
    index = lax.broadcasted_iota(jnp.int32, (STAT, width), 0)
    block = jnp.zeros((STAT, width), F32)
    for i, row in enumerate(rows):
        block = jnp.where(index == i, row, block)
    return block.astype(BF16)


def stats_of(part_ref, base, head):
    block = part_ref[base : base + STAT, :].astype(F32)
    o = 5 * head
    top = block[o : o + 1] + block[o + 1 : o + 2] + block[o + 2 : o + 3]
    total = block[o + 3 : o + 4] + block[o + 4 : o + 5]
    return top, total


def folded_softmax(done, kv, at, q):
    step = math.gcd(kv.shape[0], HD)
    parts = list(done)
    for c in range(0, kv.shape[0], step):
        s = dot(kv[c : c + step, at : at + HD], q, 1, 1)
        high = jnp.max(s, axis=0, keepdims=True)
        p = jnp.exp2((s - high) * SCORE2)
        value = dot(kv[c : c + step, at + HD : at + 2 * HD], p.astype(BF16), 0, 0)
        parts.append((high, jnp.sum(p, axis=0, keepdims=True), value))
    m = functools.reduce(jnp.maximum, [part[0] for part in parts])
    fades = [jnp.exp2((part[0] - m) * SCORE2) for part in parts]
    l = sum(f * part[1] for f, part in zip(fades, parts))
    o = sum(f * part[2] for f, part in zip(fades, parts))
    return m, l, o


def prefix_body(heads, spans, pair, *refs):
    me, owner, own, nbr = refs[:4]
    qs = refs[4 : 4 + spans]
    outs = refs[4 + spans : 4 + 2 * spans]
    kv = refs[4 + 2 * spans]
    here = owner[0] // pair == me[0] // pair
    rows = heads * HD

    @pl.when(here)
    def _():
        kv[...] = jnp.where(owner[0] == me[0], own[...], nbr[...])
        for q, out in zip(qs, outs):
            wide = Q_PER_KV * (q.shape[0] - STAT) // (2 * heads * Q_PER_KV)
            stats = []
            for h in range(heads):
                qh = q[h * wide : (h + 1) * wide, :]
                m, l, o = folded_softmax([], kv, 2 * h * HD, qh)
                out[h * HD : (h + 1) * HD, :] = o.astype(BF16)
                stats += pieces(m, 3) + pieces(l, 2)
            out[rows:, :] = stat_block(stats, wide)

    @pl.when(jnp.logical_not(here))
    def _():
        for q, out in zip(qs, outs):
            wide = out.shape[1]
            out[:rows, :] = jnp.zeros((rows, wide), BF16)
            low = jnp.full((1, wide), LOW, F32)
            zero = jnp.zeros((1, wide), F32)
            out[rows:, :] = stat_block((pieces(low, 3) + [zero, zero]) * heads, wide)


def blocks_body(last, heads, spans, slots, pair, *refs):
    me, src, blk, pool = refs[:4]
    qs = refs[4 : 4 + spans]
    refs = refs[4 + spans :]
    if last:
        before, outs, (top, tot, acc) = refs[:3], refs[3 : 3 + spans], refs[3 + spans :]
    else:
        top, tot, acc = refs
    z = me[0] // pair
    rows = heads * HD
    full = qs[0].shape[0] - STAT
    wide = acc.shape[-1]
    ctxs = [jnp.max(q[full:, :].astype(F32)) for q in qs]
    if last:
        for ref, old in zip((top, tot, acc), before):
            ref[...] = old[...]
    else:
        top[...] = jnp.full(top.shape, LOW, F32)
        tot[...] = jnp.zeros_like(tot)
        acc[...] = jnp.zeros_like(acc)
    for k, (q, ctx) in enumerate(zip(qs, ctxs)):
        reader = lax.rem(z + (spans - k), spans) * pair + lax.rem(me[0], pair)

        def slot(j, carry, k=k, q=q, reader=reader, ctx=ctx):
            source = src[reader, j]
            held = (source // pair == z) & (source != me[0]) if last else source == me[0]

            @pl.when(held & (j.astype(F32) < ctx))
            def _():
                b = blk[reader, j]
                for h in range(heads):
                    kv = pool[b, :, 2 * h * HD : 2 * (h + 1) * HD]
                    lo = full // 2 + h * wide
                    done = [(top[k, h], tot[k, h], acc[k, h])]
                    top[k, h], tot[k, h], acc[k, h] = folded_softmax(done, kv, 0, q[lo : lo + wide, :])

            return carry

        lax.fori_loop(0, slots, slot, 0)
    if last:
        for k, out in enumerate(outs):
            stats = []
            for h in range(heads):
                out[h * HD : (h + 1) * HD, :] = acc[k, h].astype(BF16)
                stats += pieces(top[k, h], 3) + pieces(tot[k, h], 2)
            out[rows:, :] = stat_block(stats, wide)


def fresh_softmax(new, r, h, q):
    fresh, wide = new.shape[1], q.shape[0]
    s = dot(new[r, :, 2 * h * HD : (2 * h + 1) * HD], q, 1, 1)
    key = lax.broadcasted_iota(jnp.int32, (fresh, wide), 0)
    token = lax.rem(lax.broadcasted_iota(jnp.int32, (fresh, wide), 1), fresh)
    seen = key <= token
    m = jnp.max(jnp.where(seen, s, LOW), axis=0, keepdims=True)
    p = jnp.where(seen, jnp.exp2((s - m) * SCORE2), 0.0)
    o = dot(new[r, :, (2 * h + 1) * HD : (2 * h + 2) * HD], p.astype(BF16), 0, 0)
    return m, jnp.sum(p, axis=0, keepdims=True), o


def join(parts):
    m = functools.reduce(jnp.maximum, [part[0] for part in parts])
    fades = [jnp.exp2((part[0] - m) * SCORE2) for part in parts]
    total = sum(f * part[1] for f, part in zip(fades, parts))
    return jnp.transpose(sum(f * part[2] for f, part in zip(fades, parts)) / total).astype(BF16)


def part_of(ref, heads, h):
    m, l = stats_of(ref, heads * HD, h)
    return m, l, ref[h * HD : (h + 1) * HD, :].astype(F32)


def join0_body(heads, spans, flag, q, new, *refs):
    parts, (out, top, tot, acc) = refs[:spans], refs[spans:]
    fresh = new.shape[1]
    wide = acc.shape[-1]
    half = heads * wide
    for h in range(heads):
        found = [fresh_softmax(new, 0, h, q[h * wide : (h + 1) * wide, :])]
        for part in parts:
            m, l, o = part_of(part, heads, h)
            found.append((jnp.where(flag[0] > 0, m, LOW), l, o))
        done = join(found)
        for g in range(Q_PER_KV):
            col = (h * Q_PER_KV + g) * HD
            out[:, col : col + HD] = done[g * fresh : (g + 1) * fresh, :]
        top[h], tot[h], acc[h] = fresh_softmax(new, 1, h, q[half + h * wide : half + (h + 1) * wide, :])


def join1_body(heads, spans, first, top, tot, acc, *refs):
    parts, out = refs[:spans], refs[spans]
    fresh = first.shape[0]
    out[0] = first[...]
    for h in range(heads):
        done = join([(top[h], tot[h], acc[h])] + [part_of(part, heads, h) for part in parts])
        for g in range(Q_PER_KV):
            col = (h * Q_PER_KV + g) * HD
            out[1, :, col : col + HD] = done[g * fresh : (g + 1) * fresh, :]


def reach(away, spans, rounds, here):
    low = high = away
    for r in range(rounds):
        odd = r % 2
        below = jnp.where((lax.rem(low, 2) != odd) & (low > 0), low - 1, low)
        above = jnp.where((lax.rem(high, 2) == odd) & (high < spans - 1), high + 1, high)
        low, high = below, above
    return (low <= here) & (here <= high)


def shared_body(spans, pair, unit, rounds, me, owner, kept, came, out):
    z, y = me[0] // pair, lax.rem(me[0], pair)
    if rounds == 0:
        take = lax.rem(owner[0], pair) != y
        base = unit
    else:
        away = owner[0] // pair
        take = jnp.logical_not(reach(away, spans, rounds - 1, z))
        base = 0
    out[...] = jnp.where(take, came[base:, :], kept[base:, :])


def state_send_body(spans, pair, unit, me, src, own, nbr, *outs):
    z, y = me[0] // pair, lax.rem(me[0], pair)
    for k, out in enumerate(outs):
        source = src[lax.rem(z + k, spans) * pair + y]
        out[...] = jnp.where(lax.rem(source, pair) == y, own[:unit, :], nbr[:unit, :])


def state_take_body(spans, pair, me, src, *refs):
    came, out = refs[:spans], refs[spans]
    z = me[0] // pair
    k1 = lax.rem(z + spans - src[me[0]] // pair, spans)
    for k in range(spans):

        @pl.when(k1 == k)
        def _(k=k):
            out[...] = came[k][...]


def silu(x):
    return x / (1.0 + jnp.exp(-x))


def gains_body(chunk, flag, st0, st1, x, w, b, wbc, out, pad):
    taps = w.shape[0]
    keep = taps - 1
    length = x.shape[1]
    lead = 8
    total = [jnp.zeros((length, wbc.shape[0]), F32) for _ in range(2)]
    for c in range(0, x.shape[2], chunk):
        at = slice(c, c + chunk)
        for r, st in enumerate((st0, st1)):
            first = st[:, at].astype(F32)
            if r == 0:
                first = jnp.where(flag[0] > 0, first, 0.0)
            pad[r, lead - keep : lead, :] = first
            pad[r, lead:, :] = x[r, :, at].astype(F32)
            acc = b[:, at] + w[0:1, at] * pad[r, lead - keep : lead - keep + length, :]
            for k in range(1, taps):
                acc = acc + w[k : k + 1, at] * pad[r, lead - keep + k : lead - keep + k + length, :]
            total[r] = total[r] + dot(silu(acc).astype(BF16), wbc[:, at], 1, 1)
    for r in range(2):
        out[r] = total[r]


def ready_body(x, dt, zg, dtb, alog, w, b, step, act, gate, dec):
    taps, length = w.shape[0], x.shape[1]
    dec[...] = jnp.exp(alog[...]) * (-LOG2E)
    for r in range(2):

        def basics(t, carry, r=r):
            raw = dt[r, t].astype(F32) + dtb[...]
            step[r, t] = jnp.maximum(raw, 0.0) + jnp.log1p(jnp.exp(-jnp.abs(raw)))
            gate[r, t] = silu(zg[r, t].astype(F32))
            return carry

        lax.fori_loop(0, length, basics, 0, unroll=4)

        def total(t, first, r=r):
            acc = b[...]
            for k in range(first, taps):
                acc = acc + w[k] * x[r, t + k - taps + 1].astype(F32)
            return acc

        for t in range(taps - 1):
            act[r, t] = total(t, taps - 1 - t)

        def later(t, carry, r=r):
            act[r, t] = silu(total(t, 0))
            return carry

        lax.fori_loop(taps - 1, length, later, 0)


def scan_body(state, flag, bc, st0, st1, step, act, gate, dec, gain, w, out):
    keep = w.shape[0] - 1
    length, sub = step.shape[1], step.shape[2]
    block = 16
    for r, st in enumerate((st0, st1)):
        for c in range(0, sub, block):
            at = slice(c, c + block)

            def held(n, r=r, st=st, at=at):
                value = st[n, at, :].astype(F32)
                return jnp.where(flag[0] > 0, value, 0.0) if r == 0 else value

            def advance(t, hs, sig, r=r, at=at):
                now = step[r, t, at, :]
                add = now * sig
                sums = [gain[at, :] * sig, None, None, None]
                after = []
                for n in range(state):
                    h = jnp.exp2(now * dec[n, at, :]) * hs[n] + bc[r * length + t, n] * add
                    term = bc[r * length + t, state + n] * h
                    i = n % 4
                    sums[i] = term if sums[i] is None else sums[i] + term
                    after.append(h)
                y = (sums[0] + sums[1]) + (sums[2] + sums[3])
                out[r, t, at, :] = (y * gate[r, t, at, :]).astype(BF16)
                return tuple(after)

            hs = tuple(held(n) for n in range(state))
            peel = keep + (length - keep) % 4
            for t in range(peel):
                sig = act[r, t, at, :]
                if t < keep:
                    for k in range(keep - t):
                        sig = sig + w[k, at, :] * held(state + t + k)
                    sig = silu(sig)
                hs = advance(t, hs, sig)

            def body(t, hs, r=r, at=at, advance=advance):
                return advance(t, hs, act[r, t, at, :])

            lax.fori_loop(peel, length, body, hs, unroll=4)


def local(
    size,
    queries,
    new_kv,
    cached_lookup_pairs,
    prefix_ssm,
    prefix_conv,
    pool_kv,
    pool_ssm,
    pool_conv,
    owner_id,
    readers,
    restore_src,
    restore_blk,
    state_src,
    ctx_blocks,
    mamba_x,
    mamba_z,
    mamba_dt,
    dt_bias,
    a_log,
    bypass_gain,
    conv_w,
    conv_b,
    w_bc,
):
    axis = "replica"
    pair = 2
    spans = size // pair
    length = queries.shape[2]
    heads = new_kv.shape[3] // (2 * HD)
    wide = Q_PER_KV * length
    slots = restore_src.shape[1]
    inner = mamba_x.shape[3]
    state = a_log.shape[0]
    keep = prefix_conv.shape[1]
    me = lax.axis_index(axis)[None]

    def across(value):
        return lax.ppermute(value, axis, [(s, s ^ 1) for s in range(size)])

    def turn(value, k):
        return lax.ppermute(value, axis, [(s, (s + k * pair) % size) for s in range(size)])

    def after(value, *others):
        return lax.optimization_barrier((value, *others))[0]

    sub = inner // HD

    def tiled(value):
        return value.reshape(value.shape[:-1] + (sub, HD))

    cols = 2 * HD
    rows = state + keep
    unit = rows * inner // cols
    states = jnp.concatenate([pool_ssm[0], pool_conv[0], prefix_ssm[0], prefix_conv[0]], axis=0)
    states = states.reshape(2 * unit, cols)
    states_nbr = across(states)

    folded = queries[0].reshape(2, length, heads * Q_PER_KV, HD).transpose(0, 2, 1, 3)
    folded = folded.reshape(2 * heads * wide, HD)
    length_rows = jnp.full((STAT, HD), ctx_blocks[0].astype(BF16), BF16)
    message = jnp.concatenate([folded, length_rows], axis=0)
    asked = [message] + [turn(message, k) for k in range(1, spans)]

    x_t, dt_t, z_t = tiled(mamba_x[0]), tiled(mamba_dt[0]), tiled(mamba_z[0])
    f32_rows = jax.ShapeDtypeStruct((2, length, sub, HD), F32)
    prepared = call(
        ready_body,
        [f32_rows] * 3 + [jax.ShapeDtypeStruct((state, sub, HD), F32)],
        [VSPEC] * 7,
    )(x_t, dt_t, z_t, tiled(dt_bias), tiled(a_log), tiled(conv_w), tiled(conv_b))
    prefix_nbr = across(cached_lookup_pairs[0])

    one = jax.ShapeDtypeStruct((unit, cols), BF16)

    def shared(rounds, kept, came):
        return call(
            functools.partial(shared_body, spans, pair, unit, rounds),
            one,
            [SSPEC] * 2 + [VSPEC] * 2,
            (),
            pl.CostEstimate(flops=50 * 10**9, bytes_accessed=150 * 10**6, transcendentals=0) if rounds == 0 else None,
        )(me, owner_id, kept, came)

    def hop(value, r):
        odd = r % 2
        near = [(i, i + 1) for i in range(odd, spans - 1, 2)]
        links = [(pair * u + j, pair * v + j) for i, n in near for u, v in ((i, n), (n, i)) for j in range(pair)]
        return lax.ppermute(value, axis, links)

    state0 = shared(0, states, states_nbr)
    hops = [hop(state0, 0)] if spans > 1 else []

    sent = call(
        functools.partial(state_send_body, spans, pair, unit),
        [one] * spans,
        [SSPEC] * 2 + [VSPEC] * 2,
        (),
        pl.CostEstimate(flops=50 * 10**9, bytes_accessed=150 * 10**6, transcendentals=0),
    )(after(me, *prepared, *asked[1:], *hops[:1]), state_src, states, states_nbr)
    came = [sent[0]] + [turn(sent[k], k) for k in range(1, spans)]
    state1 = call(
        functools.partial(state_take_body, spans, pair),
        one,
        [SSPEC] * 2 + [VSPEC] * spans,
    )(me, state_src, *came)
    part_shape = jax.ShapeDtypeStruct((heads * HD + STAT, wide), BF16)
    keys = cached_lookup_pairs.shape[1]
    part0 = call(
        functools.partial(prefix_body, heads, spans, pair),
        [part_shape] * spans,
        [SSPEC] * 2 + [VSPEC] * (2 + spans),
        [pltpu.VMEM(cached_lookup_pairs.shape[1:], BF16)],
        pl.CostEstimate(flops=10**6, bytes_accessed=10**4, transcendentals=0),
    )(me, owner_id, cached_lookup_pairs[0], prefix_nbr, *asked)
    for r in range(1, spans):
        state0 = shared(r, state0, hops[-1])
        if r < spans - 1:
            hops.append(hop(after(state0, sent[0]), r))
    got0 = [part0[0]] + [turn(after(part0[k], came[spans - k]), spans - k) for k in range(1, spans)]

    first = state * inner // cols

    def taps_of(value):
        return value[first:].reshape(keep, inner)

    chunk = math.gcd(inner, 512)
    partial = call(
        functools.partial(gains_body, chunk),
        jax.ShapeDtypeStruct((2, length, w_bc.shape[1]), F32),
        [SSPEC] + [VSPEC] * 6,
        [pltpu.VMEM((2, length + 8, chunk), F32)],
        pl.CostEstimate(flops=2 * 2 * length * inner * 32, bytes_accessed=2 << 20, transcendentals=2 * length * inner),
    )(readers, taps_of(state0), taps_of(state1), mamba_x[0], conv_w, conv_b[None], w_bc.T)
    both = partial + lax.ppermute(partial, "channel", [(0, 1), (1, 0)])
    bc = both.reshape(2 * length, w_bc.shape[1])
    pool_nbr = across(pool_kv[0])
    kept = [
        jax.ShapeDtypeStruct((spans, heads, 1, wide), F32),
        jax.ShapeDtypeStruct((spans, heads, 1, wide), F32),
        jax.ShapeDtypeStruct((spans, heads, HD, wide), F32),
    ]
    before = call(
        functools.partial(blocks_body, False, heads, spans, slots, pair),
        kept,
        [SSPEC] * 3 + [VSPEC] * (1 + spans),
    )(after(me, part0[0]), restore_src, restore_blk, pool_kv[0], *asked)
    fresh_shape = jax.ShapeDtypeStruct((length, heads * Q_PER_KV * HD), BF16)
    joined = call(
        functools.partial(join0_body, heads, spans),
        [fresh_shape] + [jax.ShapeDtypeStruct(v.shape[1:], F32) for v in kept],
        [SSPEC] + [VSPEC] * (2 + spans),
    )(readers, message, new_kv[0], *got0)
    part1 = call(
        functools.partial(blocks_body, True, heads, spans, slots, pair),
        [part_shape] * spans,
        [SSPEC] * 3 + [VSPEC] * (4 + spans),
        [pltpu.VMEM(v.shape, F32) for v in kept],
        pl.CostEstimate(flops=20 * 10**9, bytes_accessed=60 * 10**6, transcendentals=0),
    )(after(me, bc, *got0[1:]), restore_src, restore_blk, pool_nbr, *asked, *before)
    got1 = [part1[0]] + [turn(part1[k], spans - k) for k in range(1, spans)]

    scan_out = call(
        functools.partial(scan_body, state),
        jax.ShapeDtypeStruct((2, length, sub, HD), BF16),
        [SSPEC] * 2 + [VSPEC] * 8,
        (),
        pl.CostEstimate(flops=2 * length * inner * state * 6, bytes_accessed=4 << 20, transcendentals=2 * length * inner * state),
    )(readers, bc, state0.reshape(rows, sub, HD), state1.reshape(rows, sub, HD), *prepared, tiled(bypass_gain), tiled(conv_w))
    mamba_out = scan_out.reshape(1, 2, length, inner)

    attention_out = call(
        functools.partial(join1_body, heads, spans),
        jax.ShapeDtypeStruct((2,) + fresh_shape.shape, BF16),
        [VSPEC] * (4 + spans),
    )(*joined, *got1)[None]
    return (attention_out, mamba_out)


def solution(mesh):
    row = ("groups", "replica")
    placed = (
        P(row, None, None, "channel"),
        P(row, None, None, "channel"),
        P(row, None, "channel"),
        P(row, None, "channel"),
        P(row, None, "channel"),
        P(row, None, None, "channel"),
        P(row, None, "channel"),
        P(row, None, "channel"),
        P("groups"),
        P(row),
        P("groups", None),
        P("groups", None),
        P("groups"),
        P(row),
        P(row, None, None, "channel"),
        P(row, None, None, "channel"),
        P(row, None, None, "channel"),
        P("channel"),
        P(None, "channel"),
        P("channel"),
        P(None, "channel"),
        P("channel"),
        P("channel", None),
    )
    return jax.shard_map(
        functools.partial(local, mesh.shape["replica"]),
        mesh=mesh,
        in_specs=placed,
        out_specs=(P(row, None, None, "channel"), P(row, None, None, "channel")),
        check_vma=False,
    )
```
